256 devices in a mesh: row: 8 (over y, z_hi), col: 32 (over x, z_lo, core).
Axes of the slice: x: 4, y: 4, z: 8 (z_hi: 2, z_lo: 4; z = z_hi * 4 + z_lo), core: 2. Of those that a mesh axis runs over, the one named last changes fastest.
Arguments:
- features: bfloat16 [65536, 256], P(('col', 'row')), may hold values from -6 to 6
- weight: bfloat16 [256, 256], replicated, may hold values from -0.375 to 0.375
- bias_vector: float32 [256], replicated, may hold values from -3 to 3
- adjacency_tiles: bfloat16 [8, 32, 24, 512, 512], P('row', 'col'), may hold values from -0.125 to 0.125
- tile_index: int32 [8, 32, 24], P('row', 'col'), may hold values from 0 to 63, as said below
- tile_count: int32 [8, 32], P('row', 'col'), may hold values from 1 to 24, as said below
- grad_output: bfloat16 [65536, 256], P(('row', 'col')), may hold values from -6 to 6
Outputs:
- output: bfloat16 [65536, 256], P(('row', 'col'))
- grad_features: bfloat16 [65536, 256], P(('col', 'row'))
- grad_weight: float32 [256, 256], replicated
- grad_bias: float32 [256], replicated
The draws below stay inside these ranges and needn't reach their ends.
Inputs may be any that keep to these rules, and one draw needn't show every extreme that they name: `tile_index`: the 24 positions of one grid block are distinct. `tile_count`: slots of a grid block at or beyond its count hold arbitrary values that are not part of A and must be ignored.
All inputs are finite; a program needn't handle non-finite values.
Results may differ from the reference program's by a relative error of at most 0.0057.
Values may be sent and summed in bfloat16 or wider, within the bound.
A program may use at most 128 MiB of HBM per device.

```python
import math
import jax
import jax.numpy as jnp
from jax import lax

F = 256
TILE = 512
NODES = 65536
ROW_TILES = 16
COL_TILES = 4
SLOTS = 24
N_ROW = 8
N_COL = 32


def draw_tile_index(key, part):
    key = jax.random.fold_in(key, 11)
    positions = ROW_TILES * COL_TILES
    devices_all = N_ROW * N_COL
    scores = jax.random.randint(key, (devices_all, positions), 0, 1 << 20)
    offsets = jnp.arange(positions, dtype=jnp.int32)
    scores = scores * positions + offsets[None, :]
    scores = scores.at[0].set(positions - 1 - offsets).at[1].set(offsets)
    ranking = jnp.argsort(scores, axis=1, stable=True).astype(jnp.int32)
    return ranking[:, :SLOTS].reshape(N_ROW, N_COL, SLOTS)


def draw_tile_count(key, part):
    key = jax.random.fold_in(key, 12)
    first_key, second_key = jax.random.split(key)
    grid_shape = (N_ROW, N_COL)
    first_draw = jax.random.randint(first_key, grid_shape, 0, SLOTS)
    second_draw = jax.random.randint(second_key, grid_shape, 0, SLOTS)
    counts = 1 + first_draw * (second_draw + SLOTS) // (2 * SLOTS)
    counts = counts.at[0, 0].set(SLOTS).at[N_ROW - 1, N_COL - 1].set(1)
    return counts.astype(jnp.int32)


def block_levels(stream_key, extent, cuts, low, largest):
    factor_of, own = 1.0, jax.random.fold_in(stream_key, 6)
    for dim, parts in cuts:
        draws = jnp.exp(jax.random.uniform(jax.random.fold_in(own, dim), (parts,), jnp.float32, low / len(cuts), largest / len(cuts)))
        factor_of = factor_of * jnp.repeat(draws, extent[dim] // parts).reshape([-1 if axis == dim else 1 for axis in range(len(extent))])
    return factor_of


def normal_values(key, extent, spread, limit, cuts=(), kind=jnp.bfloat16):
    level = block_levels(key, extent, cuts, -0.22, 0.18) if cuts else 1.0
    entries = jax.random.normal(key, extent, jnp.float32) * spread * level
    return jnp.minimum(jnp.maximum(entries, -limit), limit).astype(kind)


def setup_inputs(seed: int = 0) -> dict:
    arg_keys = jax.random.split(jax.random.key(seed), 8)
    return {
        "features": normal_values(arg_keys[0], (NODES, F), 1.0, 6.0, ((0, 256),)),
        "weight": normal_values(arg_keys[1], (F, F), F ** -0.5, 0.375),
        "bias_vector": normal_values(arg_keys[2], (F,), 0.5, 3.0, (), jnp.float32),
        "adjacency_tiles": normal_values(arg_keys[3], (N_ROW, N_COL, SLOTS, TILE, TILE), (4 * TILE) ** -0.5, 0.125, ((0, 8), (1, 32))),
        "tile_index": draw_tile_index(jax.random.fold_in(arg_keys[7], 71), 0),
        "tile_count": draw_tile_count(jax.random.fold_in(arg_keys[7], 71), 0),
        "grad_output": normal_values(arg_keys[6], (NODES, F), 1.0, 6.0, ((0, 256),)),
    }


def silu_slope(shifted):
    sigma = jax.nn.sigmoid(shifted)
    return sigma * (1.0 + shifted * (1.0 - sigma))

def accumulate(adjacency_tiles, tile_index, tile_count, source, flipped):
    nodes = source.shape[0]
    block_rows = nodes // N_ROW
    block_cols = nodes // N_COL
    total = N_ROW * N_COL * SLOTS

    def visit(counter, running):
        counter = jnp.asarray(counter).astype(jnp.int32)
        grid_row = counter // (N_COL * SLOTS)
        grid_col = counter // SLOTS % N_COL
        position = counter % SLOTS
        matrix = adjacency_tiles[grid_row, grid_col, position]
        located = tile_index[grid_row, grid_col, position].astype(jnp.int32)
        active = position < tile_count[grid_row, grid_col]
        row_start = (grid_row * block_rows + located // COL_TILES * TILE).astype(jnp.int32)
        col_start = (grid_col * block_cols + located % COL_TILES * TILE).astype(jnp.int32)

        def add_product(current_sum):
            if flipped:
                piece = lax.dynamic_slice_in_dim(source, row_start, TILE, 0)
                product = jnp.dot(matrix.T, piece, preferred_element_type=jnp.float32)
                target = col_start
            else:
                piece = lax.dynamic_slice_in_dim(source, col_start, TILE, 0)
                product = jnp.dot(matrix, piece, preferred_element_type=jnp.float32)
                target = row_start
            current = lax.dynamic_slice_in_dim(current_sum, target, TILE, 0)
            return lax.dynamic_update_slice_in_dim(current_sum, current + product, target, 0)
        return lax.cond(active, add_product, lambda kept: kept, running)
    start = jnp.zeros((nodes, source.shape[1]), jnp.float32)
    return lax.fori_loop(0, total, visit, start)

def reference(features, weight, bias_vector, adjacency_tiles, tile_index, tile_count, grad_output):
    mapped = jnp.dot(features, weight, preferred_element_type=jnp.float32).astype(jnp.bfloat16)
    aggregated = accumulate(adjacency_tiles, tile_index, tile_count, mapped, False)
    shifted = aggregated + bias_vector[None, :]
    output = jax.nn.silu(shifted).astype(jnp.bfloat16)
    signal = (grad_output.astype(jnp.float32) * silu_slope(shifted)).astype(jnp.bfloat16)
    grad_mapped = accumulate(adjacency_tiles, tile_index, tile_count, signal, True)
    grad_features = jnp.dot(grad_mapped, weight.astype(jnp.float32).T, precision=lax.Precision.HIGHEST).astype(jnp.bfloat16)
    scale = 1.0 / math.sqrt(NODES)
    grad_weight = jnp.dot(features.astype(jnp.float32).T, grad_mapped, precision=lax.Precision.HIGHEST) * scale
    grad_bias = lax.optimization_barrier(jnp.sum(signal.astype(jnp.float32), axis=0)) * scale
    return (output, grad_features, grad_weight, grad_bias)
```

```python
import math

import jax
import jax.numpy as jnp
from jax import lax
from jax.experimental import pallas as pl
from jax.experimental.pallas import tpu as pltpu
from jax.sharding import PartitionSpec as P

MESH = pl.DeviceIdType.MESH
F32 = jnp.float32
BF16 = jnp.bfloat16
N = 256
HALF = 128
TILE = 512
SLOTS = 24
LOADS = 8


def pick(index, options):
    value = options[-1]
    for place in range(len(options) - 2, -1, -1):
        value = jnp.where(index == place, options[place], value)
    return value


def order_far_first(j, z):
    low = jnp.where(z < 2, z, 3 - z)
    base = jnp.where(low == 0, 3 - j, pick(j, [3, 0, 2, 1]))
    return jnp.where(z < 2, base, 3 - base)


def order_near_first(j, z):
    low = jnp.where(z < 2, z, 3 - z)
    base = jnp.where(low == 0, j, pick(j, [1, 0, 2, 3]))
    return jnp.where(z < 2, base, 3 - base)


def split_dot(left, right, dims):
    high = left.astype(BF16)
    low = (left - high.astype(F32)).astype(BF16)
    return lax.dot_general(high, right, dims, preferred_element_type=F32) + lax.dot_general(
        low, right, dims, preferred_element_type=F32
    )


def kernel(
    slots, features, weight, bias, tiles_hbm, cotangent,
    output, grad_features, grad_weight, grad_bias,
    tiles, feat, pair_out, pair_in, own, xa, xb, xc, xra, xrb, xrc, zs, zr,
    sig, acc, ya, yb, yc, yra, yrb, yrc, qs, qr,
    wa, wra, wk, wx, wz, wg, work,
    load_sem, fy_s, fy_r, fh_s, fh_r, pair_s, pair_r, x_s, x_r, z_s, z_r,
    gp_s, gp_r, gx_s, gx_r, gz_s, gz_r, y_s, y_r, q_s, q_r,
    wa_s, wa_r, wk_s, wk_r, wx_s, wx_r, wz_s, wz_r, wg_s, wg_r,
):
    row, col = lax.axis_index("row"), lax.axis_index("col")
    y, h = row // 2, row % 2
    x, z, k = col // 8, (col // 2) % 4, col % 2
    other = 1 - k
    scale = 1.0 / math.sqrt(65536)

    def column(xx, zz, kk):
        return (xx * 4 + zz) * 2 + kk

    def remote(src, dst, send, recv, to_row, to_col):
        return pltpu.make_async_remote_copy(
            src_ref=src, dst_ref=dst, send_sem=send, recv_sem=recv,
            device_id=(to_row, to_col), device_id_type=MESH,
        )

    x_next = [column((x + 1) % 4, z, k), column((x + 3) % 4, z, k)]
    y_next = [((y + 1) % 4) * 2 + h, ((y + 3) % 4) * 2 + h]
    z_up = column(x, jnp.minimum(z + 1, 3), k)
    z_down = column(x, jnp.maximum(z - 1, 0), k)
    z_next = [z_up, z_down]
    twin = column(x, z, other)
    across = y * 2 + 1 - h
    edge = (z == 0) | (z == 3)

    def rows(half):
        return pl.ds(half * HALF, HALF)

    barrier = pltpu.get_barrier_semaphore()
    partners = [(row, twin)]
    for step in range(1, 4):
        partners.append((row, column((x + step) % 4, z, k)))
        partners.append((row, column(x, (z + step) % 4, k)))
    for step in range(1, 8):
        partners.append(((row + step) % 8, col))
    for to_row, to_col in partners:
        pl.semaphore_signal(barrier, inc=1, device_id=(to_row, to_col), device_id_type=MESH)

    def tile_load(part):
        count = SLOTS // LOADS
        return pltpu.make_async_copy(
            tiles_hbm.at[pl.ds(part * count, count)], tiles.at[pl.ds(part * count, count)], load_sem.at[part]
        )

    for part in range(LOADS):
        tile_load(part).start()
    tiles[SLOTS] = jnp.zeros((TILE, TILE), BF16)
    acc[...] = jnp.zeros(acc.shape, F32)
    mine = pl.ds(row * N, N)
    feat[mine, :] = features[...]
    pl.semaphore_wait(barrier, len(partners))

    def feat_rows(yy, hh, half):
        return feat.at[pl.ds((yy * 2 + hh) * N + half * HALF, HALF)]

    def feat_across(half):
        here = feat_rows(y, h, half)
        return remote(here, here, fh_s.at[half], fh_r.at[half], across, col)

    def feat_across_in(half):
        there = feat_rows(y, 1 - h, half)
        return remote(there, there, fh_s.at[half], fh_r.at[half], across, col)

    def feat_y(kind, way, g):
        hh = h if g == 0 else 1 - h
        behind = (y + (3 if way == 0 else 1)) % 4
        block = feat_rows(behind if kind == 2 else y, hh, way if kind != 1 else 1 - way)
        return remote(block, block, fy_s.at[kind, way, g], fy_r.at[kind, way, g], y_next[way], col)

    def feat_y_in(kind, way, g):
        hh = h if g == 0 else 1 - h
        behind = (y + (3 if way == 0 else 1)) % 4
        source = (y + 2) % 4 if kind == 2 else behind
        block = feat_rows(source, hh, way if kind != 1 else 1 - way)
        return remote(block, block, fy_s.at[kind, way, g], fy_r.at[kind, way, g], y_next[way], col)

    for half in range(2):
        feat_across(half).start()
    for kind in range(2):
        for way in range(2):
            feat_y(kind, way, 0).start()
    for way in range(2):
        feat_y_in(0, way, 0).wait_recv()
        feat_y(2, way, 0).start()
    for half in range(2):
        feat_across_in(half).wait_recv()
        feat_y(0, half, 1).start()
        feat_y(1, 1 - half, 1).start()
    for way in range(2):
        feat_y_in(0, way, 1).wait_recv()
        feat_y(2, way, 1).start()
    for g in range(2):
        for way in range(2):
            feat_y_in(1, way, g).wait_recv()
            feat_y_in(2, way, g).wait_recv()
    for part in range(LOADS):
        tile_load(part).wait()

    def pair_copy(u):
        return remote(pair_out.at[u], pair_in.at[u], pair_s.at[u], pair_r.at[u], row, twin)

    def x_copy(kind, way, j):
        if kind == 0:
            src, dst = xa.at[j, rows(way)], xra.at[way, j]
        elif kind == 1:
            src, dst = xb.at[way, j], xrb.at[way, j]
        else:
            src, dst = xc.at[way, j], xrc.at[way, j]
        return remote(src, dst, x_s.at[kind, way, j], x_r.at[kind, way, j], row, x_next[way])

    def z_copy(j):
        target = order_far_first(j, z)
        way = jnp.where(target > z, 0, 1)
        to = jnp.where(target > z, z_up, z_down)
        return remote(zs.at[j], zr.at[way, target], z_s.at[j], z_r.at[way, target], row, to)

    def z_wait(way, target):
        block = zr.at[way, target]
        remote(zs.at[0], block, z_s.at[0], z_r.at[way, target], row, twin).wait_recv()

    def forward_half(t, k_half):
        total = None
        for c in range(4):
            part = jnp.dot(
                tiles[slots[t * 4 + c], pl.ds(k_half * N, N), :],
                feat[c * TILE : (c + 1) * TILE, :],
                preferred_element_type=F32,
            )
            total = part if total is None else total + part
        return total

    def forward_step(s, carry):
        @pl.when(s < 16)
        def _():
            xx = (x + pick(s % 4, [2, 1, 3, 0])) % 4
            t = xx * 4 + order_far_first(s // 4, z)
            pair_out[s] = forward_half(t, other).astype(BF16)
            pair_copy(s).start()
            own[s] = forward_half(t, k)

        @pl.when((s >= 1) & (s <= 16))
        def _():
            u = s - 1
            j = u // 4
            pair_copy(u).wait_recv()

            @pl.when(u % 4 == 0)
            def _():
                xa[j] = (own[u] + pair_in[u].astype(F32)).astype(BF16)
                x_copy(0, 0, j).start()
                x_copy(0, 1, j).start()

            for way in range(2):

                @pl.when(u % 4 == 1 + way)
                def _():
                    far, near = rows(way), rows(1 - way)
                    xb[way, j] = (own[u, near, :] + pair_in[u, near, :].astype(F32)).astype(BF16)
                    x_copy(1, way, j).start()
                    own[u, far, :] = own[u, far, :] + pair_in[u, far, :].astype(F32)

            @pl.when(u % 4 == 3)
            def _():
                own[u] = own[u] + pair_in[u].astype(F32)

        @pl.when((s % 4 == 0) & (s >= 4) & (s <= 16))
        def _():
            j = s // 4 - 1
            for way in range(2):
                x_copy(0, way, j).wait_recv()
                xc[way, j] = (own[4 * j + 1 + way, rows(way), :] + xra[way, j].astype(F32)).astype(BF16)
                x_copy(2, way, j).start()

        @pl.when((s % 4 == 3) & (s >= 7))
        def _():
            j = (s - 7) // 4
            u = 4 * j + 3
            for way in range(2):
                x_copy(1, way, j).wait_recv()
                x_copy(2, way, j).wait_recv()
            for half in range(2):
                own[u, rows(half), :] = (
                    own[u, rows(half), :] + xrc[half, j].astype(F32) + xrb[1 - half, j].astype(F32)
                )

            @pl.when(edge & (j < 3))
            def _():
                zs[j] = own[u].astype(BF16)
                z_copy(j).start()

            def middle(jj):
                target = order_far_first(jj, z)
                way = jnp.where(target > z, 0, 1)
                z_wait(way, target)
                zs[jj] = (own[4 * jj + 3] + zr[way, target].astype(F32)).astype(BF16)
                z_copy(jj).start()

            @pl.when(jnp.logical_not(edge) & (j == 1))
            def _():
                middle(0)

            @pl.when(jnp.logical_not(edge) & (j == 2))
            def _():
                middle(1)
                middle(2)

        return carry

    lax.fori_loop(0, 20, forward_step, 0)

    @pl.when(z > 0)
    def _():
        z_wait(0, z)
        own[15] = own[15] + zr[0, z].astype(F32)

    @pl.when(z < 3)
    def _():
        z_wait(1, z)
        own[15] = own[15] + zr[1, z].astype(F32)

    gathered = own[15]
    shifted = split_dot(gathered, weight[...], (((1,), (0,)), ((), ()))) + bias[...]
    sigma = jax.nn.sigmoid(shifted)
    output[...] = (shifted * sigma).astype(BF16)
    signal = (cotangent[...].astype(F32) * (sigma * (1.0 + shifted * (1.0 - sigma)))).astype(BF16)
    work[...] = signal
    sig[x * 4 + z, k] = signal.astype(F32).T.astype(BF16)

    def sig_pair(t, kk):
        block = sig.at[t, kk]
        return remote(block, block, gp_s.at[t], gp_r.at[t], row, twin)

    def sig_z(way, piece):
        block = sig.at[x * 4 + piece, k]
        return remote(block, block, gz_s.at[way, piece], gz_r.at[way, piece], row, z_next[way])

    def sig_x(kind, way, j, arriving=False):
        piece = order_near_first(j, z)
        behind = (x + (3 if way == 0 else 1)) % 4
        if arriving:
            source = (x + 2) % 4 if kind == 2 else behind
        else:
            source = behind if kind == 2 else x
        block = sig.at[source * 4 + piece, k, rows(way if kind != 1 else 1 - way)]
        return remote(block, block, gx_s.at[kind, way, j], gx_r.at[kind, way, j], row, x_next[way])

    def launch_piece(j):
        for kind in range(2):
            for way in range(2):
                sig_x(kind, way, j).start()
        sig_pair(x * 4 + order_near_first(j, z), k).start()

    @pl.when(z < 3)
    def _():
        sig_z(0, z).start()

    @pl.when(z > 0)
    def _():
        sig_z(1, z).start()

    launch_piece(0)

    def wa_copy(peer):
        return remote(wa.at[peer], wra.at[row], wa_s.at[peer], wa_r.at[row], peer, col)

    def wa_in(peer):
        return remote(wa.at[peer], wra.at[peer], wa_s.at[peer], wa_r.at[peer], peer, col)

    part = split_dot(gathered.T, work[...], (((1,), (0,)), ((), ())))
    bias_part = jnp.sum(work[...].astype(F32), axis=0, keepdims=True)
    bias_rows = jnp.where(lax.broadcasted_iota(jnp.int32, (8, N), 0) == 0, jnp.broadcast_to(bias_part, (8, N)), 0.0)
    for peer in range(8):
        wa[peer, 0:32, :] = part[peer * 32 : (peer + 1) * 32, :]
        wa[peer, 32:40, :] = bias_rows
    wra[row] = wa[row]
    for step in range(1, 8):
        wa_copy((row + step) % 8).start()

    def wk_copy(here):
        return remote(wk.at[here], wk.at[here], wk_s.at[0], wk_r.at[0], row, twin)

    def wx_copy(here, to):
        return remote(wx.at[here], wx.at[here], wx_s.at[to], wx_r.at[here], row, column(to, z, k))

    def wz_copy(here, to):
        return remote(wz.at[here], wz.at[here], wz_s.at[to], wz_r.at[here], row, column(x, to, k))

    def wg_copy(here, to):
        return remote(wg.at[here], wg.at[here], wg_s.at[to], wg_r.at[here], to, col)

    def total_of(ref, count):
        total = ref[0]
        for place in range(1, count):
            total = total + ref[place]
        return total

    def weights_rows():
        for step in range(1, 8):
            wa_in((row + step) % 8).wait_recv()
        wk[k] = total_of(wra, 8)
        wk_copy(k).start()

    def weights_pair():
        wk_copy(other).wait_recv()
        wx[x] = total_of(wk, 2)
        for step in range(1, 4):
            wx_copy(x, (x + step) % 4).start()

    def weights_x():
        for step in range(1, 4):
            wx_copy((x + step) % 4, (x + step) % 4).wait_recv()
        wz[z] = total_of(wx, 4)
        for step in range(1, 4):
            wz_copy(z, (z + step) % 4).start()

    def weights_z():
        for step in range(1, 4):
            wz_copy((z + step) % 4, (z + step) % 4).wait_recv()
        wg[row] = total_of(wz, 4) * scale
        for step in range(1, 8):
            wg_copy(row, (row + step) % 8).start()

    def backward_step(s, carry):
        j = s // 4
        live = s < 16

        @pl.when(live & (s % 4 == 0))
        def _():
            for way in range(2):
                sig_x(0, way, j, True).wait_recv()
                sig_x(2, way, j).start()

        @pl.when((s % 4 == 1) & (s < 12))
        def _():
            jj = j + 1
            piece = order_near_first(jj, z)

            @pl.when(z == 0)
            def _():
                sig_z(1, piece).wait_recv()

            @pl.when(z == 3)
            def _():
                sig_z(0, piece).wait_recv()

            @pl.when(jnp.logical_not(edge) & (jj == 1))
            def _():
                sig_z(0, z - 1).wait_recv()
                sig_z(0, z - 1).start()
                sig_z(1, z + 1).wait_recv()
                sig_z(1, z + 1).start()

            @pl.when((z == 1) & (jj == 2))
            def _():
                sig_z(1, 3).wait_recv()
                sig_z(1, 3).start()

            @pl.when((z == 2) & (jj == 2))
            def _():
                sig_z(0, 0).wait_recv()
                sig_z(0, 0).start()

            launch_piece(jj)

        @pl.when(live & (s % 4 == 2))
        def _():
            piece = order_near_first(j, z)
            for way in range(2):
                sig_x(1, way, j, True).wait_recv()
                sig_pair(((x + (3 if way == 0 else 1)) % 4) * 4 + piece, k).start()

        @pl.when(live & (s % 4 == 3))
        def _():
            for way in range(2):
                sig_x(2, way, j, True).wait_recv()
            sig_pair(((x + 2) % 4) * 4 + order_near_first(j, z), k).start()

        for when, what in ((4, weights_rows), (7, weights_pair), (10, weights_x), (14, weights_z)):

            @pl.when(s == when)
            def _(what=what):
                what()

        @pl.when(s >= 2)
        def _():
            u = s - 2
            t = ((x + pick(u % 4, [0, 3, 1, 2])) % 4) * 4 + order_near_first(u // 4, z)
            sig_pair(t, other).wait_recv()
            for c in range(4):
                slot = slots[t * 4 + c]
                part = jnp.dot(sig[t, 0], tiles[slot, 0:N, :], preferred_element_type=F32) + jnp.dot(
                    sig[t, 1], tiles[slot, N:TILE, :], preferred_element_type=F32
                )
                acc[c, 0] += part[:, 0:N]
                acc[c, 1] += part[:, N:TILE]

        return carry

    lax.fori_loop(0, 18, backward_step, 0)

    def y_copy(kind, way, g):
        if kind == 0:
            src, dst = ya.at[g, rows(way)], yra.at[way, g]
        elif kind == 1:
            src, dst = yb.at[way, g], yrb.at[way, g]
        else:
            src, dst = yc.at[way, g], yrc.at[way, g]
        return remote(src, dst, y_s.at[kind, way, g], y_r.at[kind, way, g], y_next[way], col)

    def y_open(g):
        hh = 1 - h if g == 0 else h
        ya[g] = acc[(y + 2) % 4, hh].astype(BF16)
        for way in range(2):
            y_copy(0, way, g).start()
        for way in range(2):
            yb[way, g] = acc[(y + (1 if way == 0 else 3)) % 4, hh, rows(1 - way), :].astype(BF16)
            y_copy(1, way, g).start()

    def y_relay(g):
        hh = 1 - h if g == 0 else h
        for way in range(2):
            y_copy(0, way, g).wait_recv()
            near = acc[(y + (1 if way == 0 else 3)) % 4, hh, rows(way), :]
            yc[way, g] = (near + yra[way, g].astype(F32)).astype(BF16)
            y_copy(2, way, g).start()

    def y_close(g):
        hh = 1 - h if g == 0 else h
        for way in range(2):
            y_copy(1, way, g).wait_recv()
            y_copy(2, way, g).wait_recv()
        for half in range(2):
            acc[y, hh, rows(half), :] = (
                acc[y, hh, rows(half), :] + yrc[half, g].astype(F32) + yrb[1 - half, g].astype(F32)
            )

    def q_copy(half):
        return remote(qs.at[half], qr.at[half], q_s.at[half], q_r.at[half], across, col)

    y_open(0)
    y_relay(0)
    y_open(1)
    y_close(0)
    for half in range(2):
        qs[half] = acc[y, 1 - h, rows(half), :].astype(BF16)
        q_copy(half).start()
    y_relay(1)
    for step in range(1, 8):
        wg_copy((row + step) % 8, (row + step) % 8).wait_recv()
    for peer in range(8):
        grad_weight[peer * 32 : (peer + 1) * 32, :] = wg[peer, 0:32, :]
    grad_bias[...] = wg[0, 32:40, :]
    y_close(1)
    for half in range(2):
        q_copy(half).wait_recv()
        acc[y, h, rows(half), :] = acc[y, h, rows(half), :] + qr[half].astype(F32)
    grad_features[...] = split_dot(acc[y, h].T, weight[...], (((1,), (1,)), ((), ()))).astype(BF16)

    for half in range(2):
        feat_across(half).wait_send()
        q_copy(half).wait_send()
    for kind in range(3):
        for way in range(2):
            for g in range(2):
                feat_y(kind, way, g).wait_send()
                y_copy(kind, way, g).wait_send()

    def sent_pair(u, carry):
        pair_copy(u).wait_send()
        sig_pair(u, k).wait_send()
        return carry

    lax.fori_loop(0, 16, sent_pair, 0)

    def sent_x(j, carry):
        for kind in range(3):
            for way in range(2):
                x_copy(kind, way, j).wait_send()
                sig_x(kind, way, j).wait_send()
        return carry

    lax.fori_loop(0, 4, sent_x, 0)
    for j in range(3):
        z_copy(j).wait_send()
    for piece in range(4):

        @pl.when((z < 3) & (piece <= z))
        def _():
            sig_z(0, piece).wait_send()

        @pl.when((z > 0) & (piece >= z))
        def _():
            sig_z(1, piece).wait_send()

    for step in range(1, 8):
        wa_copy((row + step) % 8).wait_send()
        wg_copy(row, (row + step) % 8).wait_send()
    wk_copy(k).wait_send()
    for step in range(1, 4):
        wx_copy(x, (x + step) % 4).wait_send()
        wz_copy(z, (z + step) % 4).wait_send()


def on_device(features, weight, bias_vector, adjacency_tiles, tile_index, tile_count, grad_output):
    located = tile_index[0, 0]
    places = jnp.arange(SLOTS, dtype=jnp.int32)[:, None]
    hit = (located[:, None] == jnp.arange(64, dtype=jnp.int32)[None, :]) & (places < tile_count[0, 0])
    slots = jnp.min(jnp.where(hit, places, SLOTS), axis=0)
    vmem = pl.BlockSpec(memory_space=pltpu.VMEM)
    dma = pltpu.SemaphoreType.DMA
    output, grad_features, grad_weight, grad_bias = pl.pallas_call(
        kernel,
        out_shape=(
            jax.ShapeDtypeStruct((N, N), BF16),
            jax.ShapeDtypeStruct((N, N), BF16),
            jax.ShapeDtypeStruct((N, N), F32),
            jax.ShapeDtypeStruct((8, N), F32),
        ),
        in_specs=[
            pl.BlockSpec(memory_space=pltpu.SMEM), vmem, vmem, vmem, pl.BlockSpec(memory_space=pl.ANY), vmem,
        ],
        out_specs=(vmem, vmem, vmem, vmem),
        scratch_shapes=[
            pltpu.VMEM((SLOTS + 1, TILE, TILE), BF16),
            pltpu.VMEM((8 * N, N), BF16),
            pltpu.VMEM((16, N, N), BF16),
            pltpu.VMEM((16, N, N), BF16),
            pltpu.VMEM((16, N, N), F32),
            pltpu.VMEM((4, N, N), BF16),
            pltpu.VMEM((2, 4, HALF, N), BF16),
            pltpu.VMEM((2, 4, HALF, N), BF16),
            pltpu.VMEM((2, 4, HALF, N), BF16),
            pltpu.VMEM((2, 4, HALF, N), BF16),
            pltpu.VMEM((2, 4, HALF, N), BF16),
            pltpu.VMEM((3, N, N), BF16),
            pltpu.VMEM((2, 4, N, N), BF16),
            pltpu.VMEM((16, 2, N, N), BF16),
            pltpu.VMEM((4, 2, N, N), F32),
            pltpu.VMEM((2, N, N), BF16),
            pltpu.VMEM((2, 2, HALF, N), BF16),
            pltpu.VMEM((2, 2, HALF, N), BF16),
            pltpu.VMEM((2, 2, HALF, N), BF16),
            pltpu.VMEM((2, 2, HALF, N), BF16),
            pltpu.VMEM((2, 2, HALF, N), BF16),
            pltpu.VMEM((2, HALF, N), BF16),
            pltpu.VMEM((2, HALF, N), BF16),
            pltpu.VMEM((8, 40, N), F32),
            pltpu.VMEM((8, 40, N), F32),
            pltpu.VMEM((2, 40, N), F32),
            pltpu.VMEM((4, 40, N), F32),
            pltpu.VMEM((4, 40, N), F32),
            pltpu.VMEM((8, 40, N), F32),
            pltpu.VMEM((N, N), BF16),
            dma((LOADS,)),
            dma((3, 2, 2)), dma((3, 2, 2)), dma((2,)), dma((2,)),
            dma((16,)), dma((16,)), dma((3, 2, 4)), dma((3, 2, 4)), dma((3,)), dma((2, 4)),
            dma((16,)), dma((16,)), dma((3, 2, 4)), dma((3, 2, 4)), dma((2, 4)), dma((2, 4)),
            dma((3, 2, 2)), dma((3, 2, 2)), dma((2,)), dma((2,)),
            dma((8,)), dma((8,)), dma((1,)), dma((1,)), dma((4,)), dma((4,)), dma((4,)), dma((4,)),
            dma((8,)), dma((8,)),
        ],
        compiler_params=pltpu.CompilerParams(
            collective_id=0, has_side_effects=True, vmem_limit_bytes=56 * 1024 * 1024
        ),
        name="graph_layer",
    )(slots, features, weight, bias_vector[None, :], adjacency_tiles[0, 0], grad_output)
    return output, grad_features, grad_weight, grad_bias[0]


def solution(mesh):
    return jax.shard_map(
        on_device,
        mesh=mesh,
        in_specs=(
            P(("col", "row"), None),
            P(),
            P(),
            P("row", "col", None, None, None),
            P("row", "col", None),
            P("row", "col"),
            P(("row", "col"), None),
        ),
        out_specs=(P(("row", "col"), None), P(("col", "row"), None), P(), P()),
        check_vma=False,
    )
```

```python
import math

import jax
import jax.numpy as jnp
from jax import lax
from jax.experimental import pallas as pl
from jax.experimental.pallas import tpu as pltpu
from jax.sharding import PartitionSpec as P

MESH = pl.DeviceIdType.MESH
F32 = jnp.float32
BF16 = jnp.bfloat16
N = 256
HALF = 128
TILE = 512
SLOTS = 24
LOADS = 8
LAG = 2
EARLY = 4
GAP = 3
HA = 2
HB = 5
HC = 9
HD = 13
HE = 17
RV = 3
CV = 6


def pick(index, options):
    value = options[-1]
    for place in range(len(options) - 2, -1, -1):
        value = jnp.where(index == place, options[place], value)
    return value


def order_far_first(j, z):
    low = jnp.where(z < 2, z, 3 - z)
    base = jnp.where(low == 0, 3 - j, pick(j, [3, 0, 2, 1]))
    return jnp.where(z < 2, base, 3 - base)


def order_near_first(j, z):
    low = jnp.where(z < 2, z, 3 - z)
    base = jnp.where(low == 0, j, pick(j, [1, 0, 2, 3]))
    return jnp.where(z < 2, base, 3 - base)


def split_dot(left, right, dims):
    high = left.astype(BF16)
    low = (left - high.astype(F32)).astype(BF16)
    return lax.dot_general(high, right, dims, preferred_element_type=F32) + lax.dot_general(
        low, right, dims, preferred_element_type=F32
    )


def kernel(
    slots, features, weight, bias, tiles_hbm, cotangent,
    output, grad_features, grad_weight, grad_bias,
    tiles, feat, pair_out, pair_in, xa, xb, xc, xra, xrb, xrc, zs, zr,
    sig, acc, ya, yb, yc, yra, yrb, yrc, qs, qr,
    wa, wra, wb, wk, wc, wx, wz, wd, we, wg, work, part_sums,
    weight_in, bias_in, cotangent_in, output_out, features_out, weight_out, bias_out,
    load_sem, fy_s, fy_r, fh_s, fh_r, pair_s, pair_r, x_s, x_r, z_s, z_r,
    gp_s, gp_r, gx_s, gx_r, gz_s, gz_r, y_s, y_r, q_s, q_r,
    wa_s, wa_r, wk_s, wk_r, wx_s, wx_r, wz_s, wz_r, wd_s, wd_r, we_s, we_r, wg_s, wg_r, in_sem, out_sem,
):
    row, col = lax.axis_index("row"), lax.axis_index("col")
    y, h = row // 2, row % 2
    x, z, k = col // 8, (col // 2) % 4, col % 2
    other = 1 - k
    scale = 1.0 / math.sqrt(65536)

    def column(xx, zz, kk):
        return (xx * 4 + zz) * 2 + kk

    def remote(src, dst, send, recv, to_row, to_col):
        return pltpu.make_async_remote_copy(
            src_ref=src, dst_ref=dst, send_sem=send, recv_sem=recv,
            device_id=(to_row, to_col), device_id_type=MESH,
        )

    x_next = [column((x + 1) % 4, z, k), column((x + 3) % 4, z, k)]
    y_next = [((y + 1) % 4) * 2 + h, ((y + 3) % 4) * 2 + h]
    z_up = column(x, jnp.minimum(z + 1, 3), k)
    z_down = column(x, jnp.maximum(z - 1, 0), k)
    z_next = [z_up, z_down]
    twin = column(x, z, other)
    across = y * 2 + 1 - h
    edge = (z == 0) | (z == 3)

    def rows(half):
        return pl.ds(half * HALF, HALF)

    barrier = pltpu.get_barrier_semaphore()
    partners = [(row, twin)]
    for step in range(1, 4):
        partners.append((row, column((x + step) % 4, z, k)))
        partners.append((((y + step) % 4) * 2 + h, col))
    for step in range(1, 8):
        place = (h * 4 + z + step) % 8
        partners.append((y * 2 + place // 4, column(x, place % 4, k)))
    for to_row, to_col in partners:
        pl.semaphore_signal(barrier, inc=1, device_id=(to_row, to_col), device_id_type=MESH)

    def tile_load(part):
        count = SLOTS // LOADS
        return pltpu.make_async_copy(
            tiles_hbm.at[pl.ds(part * count, count)], tiles.at[pl.ds(part * count, count)], load_sem.at[part]
        )

    def load(part):
        src, dst = ((weight, weight_in), (bias, bias_in), (cotangent, cotangent_in))[part]
        return pltpu.make_async_copy(src, dst, in_sem.at[part])

    def output_store():
        return pltpu.make_async_copy(output_out, output, out_sem.at[0])

    def features_store():
        return pltpu.make_async_copy(features_out, grad_features, out_sem.at[1])

    def weight_store():
        return pltpu.make_async_copy(weight_out, grad_weight, out_sem.at[2])

    def bias_store():
        return pltpu.make_async_copy(bias_out, grad_bias, out_sem.at[3])

    mine = pltpu.make_async_copy(features, feat.at[pl.ds(row * N, N)], in_sem.at[3])
    mine.start()
    for part in range(LOADS):
        tile_load(part).start()
    for part in range(3):
        load(part).start()
    mine.wait()
    pl.semaphore_wait(barrier, len(partners))

    def feat_rows(yy, hh, half):
        return feat.at[pl.ds((yy * 2 + hh) * N + half * HALF, HALF)]

    def feat_across(half):
        here = feat_rows(y, h, half)
        return remote(here, here, fh_s.at[half], fh_r.at[half], across, col)

    def feat_across_in(half):
        there = feat_rows(y, 1 - h, half)
        return remote(there, there, fh_s.at[half], fh_r.at[half], across, col)

    def feat_y(kind, way, g):
        hh = h if g == 0 else 1 - h
        behind = (y + (3 if way == 0 else 1)) % 4
        block = feat_rows(behind if kind == 2 else y, hh, way if kind != 1 else 1 - way)
        return remote(block, block, fy_s.at[kind, way, g], fy_r.at[kind, way, g], y_next[way], col)

    def feat_y_in(kind, way, g):
        hh = h if g == 0 else 1 - h
        behind = (y + (3 if way == 0 else 1)) % 4
        source = (y + 2) % 4 if kind == 2 else behind
        block = feat_rows(source, hh, way if kind != 1 else 1 - way)
        return remote(block, block, fy_s.at[kind, way, g], fy_r.at[kind, way, g], y_next[way], col)

    for half in range(2):
        feat_across(half).start()
    for way in range(2):
        feat_y(0, way, 0).start()
    tiles[SLOTS] = jnp.zeros((TILE, TILE), BF16)
    acc[...] = jnp.zeros(acc.shape, F32)
    for way in range(2):
        feat_y(0, way, 0).wait_send()
    for way in range(2):
        feat_y(1, way, 0).start()
    for way in range(2):
        feat_y_in(0, way, 0).wait_recv()
        feat_y(2, way, 0).start()
    for way in range(2):
        feat_y_in(1, way, 0).wait_recv()
        feat_y_in(2, way, 0).wait_recv()
    for part in range(LOADS):
        tile_load(part).wait()

    def row_tile(s):
        xx = (x + pick(s % 4, [2, 1, 3, 0])) % 4
        return xx * 4 + order_far_first(s // 4, z)

    def forward_half(t, k_half, hh):
        total = None
        lanes = pl.ds(pl.multiple_of(hh * N, N), N)
        for c in range(4):
            part = jnp.dot(
                tiles[slots[t * 4 + c], pl.ds(pl.multiple_of(k_half * N, N), N), lanes],
                feat[pl.ds(pl.multiple_of((c * 2 + hh) * N, N), N), :],
                preferred_element_type=F32,
            )
            total = part if total is None else total + part
        return total

    def early_step(s, carry):
        @pl.when(s == EARLY)
        def _():
            for half in range(2):
                feat_across_in(half).wait_recv()
                feat_y(0, half, 1).start()

        @pl.when(s == EARLY + GAP)
        def _():
            for way in range(2):
                feat_y(1, way, 1).start()

        @pl.when(s == EARLY + GAP + 2)
        def _():
            for way in range(2):
                feat_y_in(0, way, 1).wait_recv()
                feat_y(2, way, 1).start()

        t = row_tile(s)
        part_sums[s, 0] = forward_half(t, other, h)
        part_sums[s, 1] = forward_half(t, k, h)
        return carry

    lax.fori_loop(0, 16, early_step, 0)
    for way in range(2):
        feat_y_in(1, way, 1).wait_recv()
        feat_y_in(2, way, 1).wait_recv()

    def pair_copy(u):
        return remote(pair_out.at[u], pair_in.at[u], pair_s.at[u], pair_r.at[u], row, twin)

    def x_copy(kind, way, j):
        if kind == 0:
            src, dst = xa.at[j, rows(way)], xra.at[way, j]
        elif kind == 1:
            src, dst = xb.at[way, j], xrb.at[way, j]
        else:
            src, dst = xc.at[way, j], xrc.at[way, j]
        return remote(src, dst, x_s.at[kind, way, j], x_r.at[kind, way, j], row, x_next[way])

    def z_copy(j):
        target = order_far_first(j, z)
        way = jnp.where(target > z, 0, 1)
        to = jnp.where(target > z, z_up, z_down)
        return remote(zs.at[j], zr.at[way, target], z_s.at[j], z_r.at[way, target], row, to)

    def z_wait(way, target):
        block = zr.at[way, target]
        remote(zs.at[0], block, z_s.at[0], z_r.at[way, target], row, twin).wait_recv()

    def relay(j):
        for way in range(2):
            x_copy(0, way, j).wait_recv()
            xc[way, j] = (part_sums[4 * j + 1 + way, 1, rows(way), :] + xra[way, j].astype(F32)).astype(BF16)
            x_copy(2, way, j).start()

    def collect(j):
        u = 4 * j + 3
        for way in range(2):
            x_copy(1, way, j).wait_recv()
            x_copy(2, way, j).wait_recv()
        for half in range(2):
            part_sums[u, 1, rows(half), :] = (
                part_sums[u, 1, rows(half), :] + xrc[half, j].astype(F32) + xrb[1 - half, j].astype(F32)
            )

        @pl.when(edge & (j < 3))
        def _():
            zs[j] = part_sums[u, 1].astype(BF16)
            z_copy(j).start()

        def middle(jj):
            target = order_far_first(jj, z)
            way = jnp.where(target > z, 0, 1)
            z_wait(way, target)
            zs[jj] = (part_sums[4 * jj + 3, 1] + zr[way, target].astype(F32)).astype(BF16)
            z_copy(jj).start()

        @pl.when(jnp.logical_not(edge) & (j == 1))
        def _():
            middle(0)

        @pl.when(jnp.logical_not(edge) & (j == 2))
        def _():
            middle(1)
            middle(2)

    def forward_step(s, carry):
        @pl.when(s < 16)
        def _():
            t = row_tile(s)
            pair_out[s] = (part_sums[s, 0] + forward_half(t, other, 1 - h)).astype(BF16)
            pair_copy(s).start()
            part_sums[s, 1] = part_sums[s, 1] + forward_half(t, k, 1 - h)

        @pl.when((s >= LAG) & (s < 16 + LAG))
        def _():
            u = s - LAG
            j = u // 4
            pair_copy(u).wait_recv()

            @pl.when(u % 4 == 0)
            def _():
                xa[j] = (part_sums[u, 1] + pair_in[u].astype(F32)).astype(BF16)
                x_copy(0, 0, j).start()
                x_copy(0, 1, j).start()

            for way in range(2):

                @pl.when(u % 4 == 1 + way)
                def _():
                    far, near = rows(way), rows(1 - way)
                    xb[way, j] = (part_sums[u, 1, near, :] + pair_in[u, near, :].astype(F32)).astype(BF16)
                    x_copy(1, way, j).start()
                    part_sums[u, 1, far, :] = part_sums[u, 1, far, :] + pair_in[u, far, :].astype(F32)

            @pl.when(u % 4 == 3)
            def _():
                part_sums[u, 1] = part_sums[u, 1] + pair_in[u].astype(F32)

        v = s - LAG - RV

        @pl.when((v >= 0) & (v < 16) & (v % 4 == 0))
        def _():
            relay(v // 4)

        w = s - LAG - CV

        @pl.when((w >= 0) & (w % 4 == 0))
        def _():
            collect(w // 4)

        return carry

    lax.fori_loop(0, LAG + CV + 13, forward_step, 0)

    @pl.when(z > 0)
    def _():
        z_wait(0, z)
        part_sums[15, 1] = part_sums[15, 1] + zr[0, z].astype(F32)

    @pl.when(z < 3)
    def _():
        z_wait(1, z)
        part_sums[15, 1] = part_sums[15, 1] + zr[1, z].astype(F32)

    gathered = part_sums[15, 1]
    for part in range(3):
        load(part).wait()
    shifted = split_dot(gathered, weight_in[...], (((1,), (0,)), ((), ()))) + bias_in[...]
    sigma = jax.nn.sigmoid(shifted)
    output_out[...] = (shifted * sigma).astype(BF16)
    output_store().start()
    signal = (cotangent_in[...].astype(F32) * (sigma * (1.0 + shifted * (1.0 - sigma)))).astype(BF16)
    work[...] = signal
    sig[x * 4 + z, k] = signal.astype(F32).T.astype(BF16)

    def sig_pair(t, kk):
        block = sig.at[t, kk]
        return remote(block, block, gp_s.at[t], gp_r.at[t], row, twin)

    def sig_z(way, piece):
        block = sig.at[x * 4 + piece, k]
        return remote(block, block, gz_s.at[way, piece], gz_r.at[way, piece], row, z_next[way])

    def sig_x(kind, way, j, arriving=False):
        piece = order_near_first(j, z)
        behind = (x + (3 if way == 0 else 1)) % 4
        if arriving:
            source = (x + 2) % 4 if kind == 2 else behind
        else:
            source = behind if kind == 2 else x
        block = sig.at[source * 4 + piece, k, rows(way if kind != 1 else 1 - way)]
        return remote(block, block, gx_s.at[kind, way, j], gx_r.at[kind, way, j], row, x_next[way])

    def launch_piece(j):
        for kind in range(2):
            for way in range(2):
                sig_x(kind, way, j).start()
        sig_pair(x * 4 + order_near_first(j, z), k).start()

    for way in range(2):
        sig_x(0, way, 0).start()

    @pl.when(z < 3)
    def _():
        sig_z(0, z).start()

    @pl.when(z > 0)
    def _():
        sig_z(1, z).start()

    sig_pair(x * 4 + z, k).start()

    def wa_copy(to, here):
        return remote(wa.at[to], wra.at[here], wa_s.at[to], wa_r.at[here], to * 2 + h, col)

    def wk_copy():
        return remote(wb.at[other], wk, wk_s.at[0], wk_r.at[0], row, twin)

    def wx_copy(to, here):
        return remote(wc.at[to], wx.at[here], wx_s.at[to], wx_r.at[here], row, column(to, z, k))

    def wz_copy(to, here):
        return remote(
            wz.at[here], wz.at[here], wz_s.at[to], wz_r.at[here], y * 2 + to // 4, column(x, to % 4, k)
        )

    def wd_copy(to, here):
        return remote(wd.at[here], wd.at[here], wd_s.at[to], wd_r.at[here], row, column(to, z, k))

    def we_copy(here):
        return remote(we.at[here], we.at[here], we_s.at[0], we_r.at[0], row, twin)

    def wg_copy(to, here):
        return remote(wg.at[here], wg.at[here], wg_s.at[to], wg_r.at[here], to * 2 + h, col)

    def total_of(ref, count):
        total = ref[0]
        for place in range(1, count):
            total = total + ref[place]
        return total

    place8 = h * 4 + z

    part = split_dot(gathered.T, work[...], (((1,), (0,)), ((), ())))
    bias_part = jnp.sum(work[...].astype(F32), axis=0, keepdims=True)
    line = lax.broadcasted_iota(jnp.int32, (8, HALF), 0)
    bias_block = jnp.where(line == 0, jnp.broadcast_to(bias_part[:, 0:HALF], (8, HALF)), 0.0) + jnp.where(
        line == 1, jnp.broadcast_to(bias_part[:, HALF:N], (8, HALF)), 0.0
    )
    for piece in range(32):
        wa[piece // 8, piece // 4 % 2, piece % 4, :, 0:N] = part[piece * 8 : piece * 8 + 8, :]
        wa[piece // 8, piece // 4 % 2, piece % 4, :, N : N + HALF] = bias_block
    for way in range(2):
        sig_x(1, way, 0).start()
    for step in range(1, 4):
        wa_copy((y + step) % 4, y).start()
    wra[y] = wa[y]

    def weights_rows():
        for step in range(1, 4):
            wa_copy((y + step) % 4, (y + step) % 4).wait_recv()
        wb[...] = total_of(wra, 4)
        wk_copy().start()

    def weights_pair():
        wk_copy().wait_recv()
        wc[...] = wb[k] + wk[...]
        for step in range(1, 4):
            wx_copy((x + step) % 4, x).start()
        wx[x] = wc[x]

    def weights_x():
        for step in range(1, 4):
            wx_copy((x + step) % 4, (x + step) % 4).wait_recv()
        wz[place8] = total_of(wx, 4)
        for step in range(1, 8):
            wz_copy((place8 + step) % 8, place8).start()

    def weights_z():
        for step in range(1, 8):
            wz_copy((place8 + step) % 8, (place8 + step) % 8).wait_recv()
        wd[x] = total_of(wz, 8) * scale
        for step in range(1, 4):
            wd_copy((x + step) % 4, x).start()

    def weights_back():
        for step in range(1, 4):
            wd_copy((x + step) % 4, (x + step) % 4).wait_recv()
        we[k] = wd[...]
        we_copy(k).start()

    def weights_twin():
        we_copy(other).wait_recv()
        wg[y] = we[...]
        for step in range(1, 4):
            wg_copy((y + step) % 4, y).start()

    def weights_end():
        for step in range(1, 4):
            wg_copy((y + step) % 4, (y + step) % 4).wait_recv()
        for piece in range(32):
            weight_out[piece * 8 : piece * 8 + 8, :] = wg[piece // 8, piece // 4 % 2, piece % 4, :, 0:N]
        bias_out[0:1, 0:HALF] = wg[0, 0, 0, 0:1, N : N + HALF]
        bias_out[0:1, HALF:N] = wg[0, 0, 0, 1:2, N : N + HALF]
        weight_store().start()
        bias_store().start()

    def relay_signal(j):
        for way in range(2):
            sig_x(0, way, j, True).wait_recv()
            sig_x(2, way, j).start()

    def next_piece(jj):
        piece = order_near_first(jj, z)

        @pl.when(z == 0)
        def _():
            sig_z(1, piece).wait_recv()

        @pl.when(z == 3)
        def _():
            sig_z(0, piece).wait_recv()

        @pl.when(jnp.logical_not(edge) & (jj == 1))
        def _():
            sig_z(0, z - 1).wait_recv()
            sig_z(0, z - 1).start()
            sig_z(1, z + 1).wait_recv()
            sig_z(1, z + 1).start()

        @pl.when((z == 1) & (jj == 2))
        def _():
            sig_z(1, 3).wait_recv()
            sig_z(1, 3).start()

        @pl.when((z == 2) & (jj == 2))
        def _():
            sig_z(0, 0).wait_recv()
            sig_z(0, 0).start()

        launch_piece(jj)

    def backward_step(s, carry):
        j = s // 4

        @pl.when(s == 0)
        def _():
            relay_signal(0)
            next_piece(1)

        @pl.when((s == 4) | (s == 8))
        def _():
            next_piece(j + 1)

        @pl.when((s % 4 == 0) & (s >= 4) & (s < 16))
        def _():
            relay_signal(j)

        @pl.when((s % 4 == 0) & (s >= 4))
        def _():
            for way in range(2):
                sig_x(2, way, j - 1, True).wait_recv()
            sig_pair(((x + 2) % 4) * 4 + order_near_first(j - 1, z), k).start()

        @pl.when((s % 4 == 1) & (s < 16))
        def _():
            piece = order_near_first(j, z)
            for way in range(2):
                sig_x(1, way, j, True).wait_recv()
                sig_pair(((x + (3 if way == 0 else 1)) % 4) * 4 + piece, k).start()

        for when, what in (
            (HA, weights_rows), (HB, weights_pair), (HC, weights_x), (HD, weights_z), (HE, weights_back),
        ):

            @pl.when(s == when)
            def _(what=what):
                what()

        last = s % 4 == 1

        @pl.when((s != 1) & (s != 16))
        def _():
            jj = jnp.where(last, j - 1, j)
            shift = pick(s % 4, [0, 2, 3, 1])
            t = ((x + shift) % 4) * 4 + order_near_first(jj, z)
            sig_pair(t, other).wait_recv()
            for c in range(4):
                slot = slots[t * 4 + c]
                part = jnp.dot(sig[t, 0], tiles[slot, 0:N, :], preferred_element_type=F32) + jnp.dot(
                    sig[t, 1], tiles[slot, N:TILE, :], preferred_element_type=F32
                )
                acc[c, 0] += part[:, 0:N]
                acc[c, 1] += part[:, N:TILE]

        return carry

    lax.fori_loop(0, 18, backward_step, 0)

    def y_copy(kind, way, g):
        if kind == 0:
            src, dst = ya.at[g, rows(way)], yra.at[way, g]
        elif kind == 1:
            src, dst = yb.at[way, g], yrb.at[way, g]
        else:
            src, dst = yc.at[way, g], yrc.at[way, g]
        return remote(src, dst, y_s.at[kind, way, g], y_r.at[kind, way, g], y_next[way], col)

    def y_open(g):
        hh = 1 - h if g == 0 else h
        ya[g] = acc[(y + 2) % 4, hh].astype(BF16)
        for way in range(2):
            y_copy(0, way, g).start()
        if g == 0:
            for way in range(2):
                y_copy(0, way, 0).wait_send()
        for way in range(2):
            yb[way, g] = acc[(y + (1 if way == 0 else 3)) % 4, hh, rows(1 - way), :].astype(BF16)
            y_copy(1, way, g).start()

    def y_relay(g):
        hh = 1 - h if g == 0 else h
        for way in range(2):
            y_copy(0, way, g).wait_recv()
            near = acc[(y + (1 if way == 0 else 3)) % 4, hh, rows(way), :]
            yc[way, g] = (near + yra[way, g].astype(F32)).astype(BF16)
            y_copy(2, way, g).start()

    def y_close(g):
        hh = 1 - h if g == 0 else h
        for way in range(2):
            y_copy(1, way, g).wait_recv()
            y_copy(2, way, g).wait_recv()
        for half in range(2):
            acc[y, hh, rows(half), :] = (
                acc[y, hh, rows(half), :] + yrc[half, g].astype(F32) + yrb[1 - half, g].astype(F32)
            )

    def q_copy(half):
        return remote(qs.at[half], qr.at[half], q_s.at[half], q_r.at[half], across, col)

    y_open(0)
    y_relay(0)
    for way in range(2):
        y_copy(2, way, 0).wait_send()
    y_open(1)
    weights_twin()
    y_close(0)
    for half in range(2):
        qs[half] = acc[y, 1 - h, rows(half), :].astype(BF16)
        q_copy(half).start()
    y_relay(1)
    y_close(1)
    weights_end()
    for half in range(2):
        q_copy(half).wait_recv()
        acc[y, h, rows(half), :] = acc[y, h, rows(half), :] + qr[half].astype(F32)
    features_out[...] = split_dot(acc[y, h].T, weight_in[...], (((1,), (1,)), ((), ()))).astype(BF16)
    features_store().start()


    for half in range(2):
        feat_across(half).wait_send()
        q_copy(half).wait_send()
    for kind in range(3):
        for way in range(2):
            for g in range(2):
                if (kind, g) != (0, 0):
                    feat_y(kind, way, g).wait_send()
                if g == 1 or kind == 1:
                    y_copy(kind, way, g).wait_send()

    def sent_pair(u, carry):
        pair_copy(u).wait_send()
        sig_pair(u, k).wait_send()
        return carry

    lax.fori_loop(0, 16, sent_pair, 0)

    def sent_x(j, carry):
        for kind in range(3):
            for way in range(2):
                x_copy(kind, way, j).wait_send()
                sig_x(kind, way, j).wait_send()
        return carry

    lax.fori_loop(0, 4, sent_x, 0)
    for j in range(3):
        z_copy(j).wait_send()
    for piece in range(4):

        @pl.when((z < 3) & (piece <= z))
        def _():
            sig_z(0, piece).wait_send()

        @pl.when((z > 0) & (piece >= z))
        def _():
            sig_z(1, piece).wait_send()

    for step in range(1, 4):
        wa_copy((y + step) % 4, y).wait_send()
        wx_copy((x + step) % 4, x).wait_send()
        wd_copy((x + step) % 4, x).wait_send()
        wg_copy((y + step) % 4, y).wait_send()
    for step in range(1, 8):
        wz_copy((place8 + step) % 8, place8).wait_send()
    wk_copy().wait_send()
    we_copy(k).wait_send()
    output_store().wait()
    weight_store().wait()
    bias_store().wait()
    features_store().wait()


def hand_over(output, grad_features, grad_weight, grad_bias, output_to, features_to, weight_to, bias_to):
    output_to[...] = output[...]
    features_to[...] = grad_features[...]
    weight_to[...] = grad_weight[...]
    bias_to[...] = grad_bias[...]


def on_device(features, weight, bias_vector, adjacency_tiles, tile_index, tile_count, grad_output):
    located = tile_index[0, 0]
    places = jnp.arange(SLOTS, dtype=jnp.int32)[:, None]
    hit = (located[:, None] == jnp.arange(64, dtype=jnp.int32)[None, :]) & (places < tile_count[0, 0])
    slots = jnp.min(jnp.where(hit, places, SLOTS), axis=0)
    vmem = pl.BlockSpec(memory_space=pltpu.VMEM)
    anywhere = pl.BlockSpec(memory_space=pl.ANY)
    dma = pltpu.SemaphoreType.DMA
    output, grad_features, grad_weight, grad_bias = pl.pallas_call(
        kernel,
        out_shape=(
            jax.ShapeDtypeStruct((N, N), BF16),
            jax.ShapeDtypeStruct((N, N), BF16),
            jax.ShapeDtypeStruct((N, N), F32),
            jax.ShapeDtypeStruct((1, N), F32),
        ),
        in_specs=[
            pl.BlockSpec(memory_space=pltpu.SMEM), anywhere, anywhere, anywhere, anywhere, anywhere,
        ],
        out_specs=(anywhere, anywhere, anywhere, anywhere),
        scratch_shapes=[
            pltpu.VMEM((SLOTS + 1, TILE, TILE), BF16),
            pltpu.VMEM((8 * N, N), BF16),
            pltpu.VMEM((16, N, N), BF16),
            pltpu.VMEM((16, N, N), BF16),
            pltpu.VMEM((4, N, N), BF16),
            pltpu.VMEM((2, 4, HALF, N), BF16),
            pltpu.VMEM((2, 4, HALF, N), BF16),
            pltpu.VMEM((2, 4, HALF, N), BF16),
            pltpu.VMEM((2, 4, HALF, N), BF16),
            pltpu.VMEM((2, 4, HALF, N), BF16),
            pltpu.VMEM((3, N, N), BF16),
            pltpu.VMEM((2, 4, N, N), BF16),
            pltpu.VMEM((16, 2, N, N), BF16),
            pltpu.VMEM((4, 2, N, N), F32),
            pltpu.VMEM((2, N, N), BF16),
            pltpu.VMEM((2, 2, HALF, N), BF16),
            pltpu.VMEM((2, 2, HALF, N), BF16),
            pltpu.VMEM((2, 2, HALF, N), BF16),
            pltpu.VMEM((2, 2, HALF, N), BF16),
            pltpu.VMEM((2, 2, HALF, N), BF16),
            pltpu.VMEM((2, HALF, N), BF16),
            pltpu.VMEM((2, HALF, N), BF16),
            pltpu.VMEM((4, 2, 4, 8, N + HALF), F32),
            pltpu.VMEM((4, 2, 4, 8, N + HALF), F32),
            pltpu.VMEM((2, 4, 8, N + HALF), F32),
            pltpu.VMEM((4, 8, N + HALF), F32),
            pltpu.VMEM((4, 8, N + HALF), F32),
            pltpu.VMEM((4, 8, N + HALF), F32),
            pltpu.VMEM((8, 8, N + HALF), F32),
            pltpu.VMEM((4, 8, N + HALF), F32),
            pltpu.VMEM((2, 4, 8, N + HALF), F32),
            pltpu.VMEM((4, 2, 4, 8, N + HALF), F32),
            pltpu.VMEM((N, N), BF16),
            pltpu.VMEM((16, 2, N, N), F32),
            pltpu.VMEM((N, N), BF16),
            pltpu.VMEM((1, N), F32),
            pltpu.VMEM((N, N), BF16),
            pltpu.VMEM((N, N), BF16),
            pltpu.VMEM((N, N), BF16),
            pltpu.VMEM((N, N), F32),
            pltpu.VMEM((1, N), F32),
            dma((LOADS,)),
            dma((3, 2, 2)), dma((3, 2, 2)), dma((2,)), dma((2,)),
            dma((16,)), dma((16,)), dma((3, 2, 4)), dma((3, 2, 4)), dma((3,)), dma((2, 4)),
            dma((16,)), dma((16,)), dma((3, 2, 4)), dma((3, 2, 4)), dma((2, 4)), dma((2, 4)),
            dma((3, 2, 2)), dma((3, 2, 2)), dma((2,)), dma((2,)),
            dma((4,)), dma((4,)), dma((1,)), dma((1,)), dma((4,)), dma((4,)), dma((8,)), dma((8,)),
            dma((4,)), dma((4,)), dma((1,)), dma((1,)), dma((4,)), dma((4,)), dma((4,)), dma((4,)),
        ],
        compiler_params=pltpu.CompilerParams(
            collective_id=0, has_side_effects=True, vmem_limit_bytes=56 * 1024 * 1024
        ),
        name="graph_layer",
    )(slots, features, weight, bias_vector[None, :], adjacency_tiles[0, 0], grad_output)
    output, grad_features, grad_weight, grad_bias = pl.pallas_call(
        hand_over,
        out_shape=(
            jax.ShapeDtypeStruct((N, N), BF16),
            jax.ShapeDtypeStruct((N, N), BF16),
            jax.ShapeDtypeStruct((N, N), F32),
            jax.ShapeDtypeStruct((1, N), F32),
        ),
        in_specs=[vmem, vmem, vmem, vmem],
        out_specs=(vmem, vmem, vmem, vmem),
        name="hand_over",
    )(output, grad_features, grad_weight, grad_bias)
    return output, grad_features, grad_weight, grad_bias[0]


def solution(mesh):
    return jax.shard_map(
        on_device,
        mesh=mesh,
        in_specs=(
            P(("col", "row"), None),
            P(),
            P(),
            P("row", "col", None, None, None),
            P("row", "col", None),
            P("row", "col"),
            P(("row", "col"), None),
        ),
        out_specs=(P(("row", "col"), None), P(("col", "row"), None), P(), P()),
        check_vma=False,
    )
```

```python
import math

import jax
import jax.numpy as jnp
from jax import lax
from jax.experimental import pallas as pl
from jax.experimental.pallas import tpu as pltpu
from jax.sharding import PartitionSpec as P

MESH = pl.DeviceIdType.MESH
F32 = jnp.float32
BF16 = jnp.bfloat16
N = 256
HALF = 128
TILE = 512
SLOTS = 24
LOADS = 8
LAG = 2
EARLY = 4
GAP = 3
HA = 2
HB = 5
HC = 9
HD = 13
HE = 17
RV = 3
CV = 6


def pick(index, options):
    value = options[-1]
    for place in range(len(options) - 2, -1, -1):
        value = jnp.where(index == place, options[place], value)
    return value


def order_far_first(j, z):
    low = jnp.where(z < 2, z, 3 - z)
    base = jnp.where(low == 0, 3 - j, pick(j, [3, 0, 2, 1]))
    return jnp.where(z < 2, base, 3 - base)


def order_near_first(j, z):
    low = jnp.where(z < 2, z, 3 - z)
    base = jnp.where(low == 0, j, pick(j, [1, 0, 2, 3]))
    return jnp.where(z < 2, base, 3 - base)


def split_dot(left, right, dims):
    high = left.astype(BF16)
    low = (left - high.astype(F32)).astype(BF16)
    return lax.dot_general(high, right, dims, preferred_element_type=F32) + lax.dot_general(
        low, right, dims, preferred_element_type=F32
    )


def kernel(
    located, limit, features, weight, bias, tiles_hbm, cotangent,
    output, grad_features, grad_weight, grad_bias,
    tiles, feat, pair_out, pair_in, xa, xb, xc, xra, xrb, xrc, zs, zr,
    sig, acc, ya, yb, yc, yra, yrb, yrc, qs, qr,
    wa, wra, wb, wk, wc, wx, wz, wd, we, wg, work, part_sums,
    weight_in, bias_in, cotangent_in, output_out, features_out, weight_out, bias_out,
    load_sem, fy_s, fy_r, fh_s, fh_r, pair_s, pair_r, x_s, x_r, z_s, z_r,
    gp_s, gp_r, gx_s, gx_r, gz_s, gz_r, y_s, y_r, q_s, q_r,
    wa_s, wa_r, wk_s, wk_r, wx_s, wx_r, wz_s, wz_r, wd_s, wd_r, we_s, we_r, wg_s, wg_r, in_sem, out_sem, slots,
):
    row, col = lax.axis_index("row"), lax.axis_index("col")
    y, h = row // 2, row % 2
    x, z, k = col // 8, (col // 2) % 4, col % 2
    other = 1 - k
    scale = 1.0 / math.sqrt(65536)

    def column(xx, zz, kk):
        return (xx * 4 + zz) * 2 + kk

    def remote(src, dst, send, recv, to_row, to_col):
        return pltpu.make_async_remote_copy(
            src_ref=src, dst_ref=dst, send_sem=send, recv_sem=recv,
            device_id=(to_row, to_col), device_id_type=MESH,
        )

    x_next = [column((x + 1) % 4, z, k), column((x + 3) % 4, z, k)]
    y_next = [((y + 1) % 4) * 2 + h, ((y + 3) % 4) * 2 + h]
    z_up = column(x, jnp.minimum(z + 1, 3), k)
    z_down = column(x, jnp.maximum(z - 1, 0), k)
    z_next = [z_up, z_down]
    twin = column(x, z, other)
    across = y * 2 + 1 - h
    edge = (z == 0) | (z == 3)

    def rows(half):
        return pl.ds(half * HALF, HALF)

    barrier = pltpu.get_barrier_semaphore()
    partners = [(row, twin)]
    for step in range(1, 4):
        partners.append((row, column((x + step) % 4, z, k)))
        partners.append((((y + step) % 4) * 2 + h, col))
    for step in range(1, 8):
        place = (h * 4 + z + step) % 8
        partners.append((y * 2 + place // 4, column(x, place % 4, k)))
    for to_row, to_col in partners:
        pl.semaphore_signal(barrier, inc=1, device_id=(to_row, to_col), device_id_type=MESH)

    def tile_load(part):
        count = SLOTS // LOADS
        return pltpu.make_async_copy(
            tiles_hbm.at[pl.ds(part * count, count)], tiles.at[pl.ds(part * count, count)], load_sem.at[part]
        )

    def load(part):
        src, dst = ((weight, weight_in), (bias, bias_in), (cotangent, cotangent_in))[part]
        return pltpu.make_async_copy(src, dst, in_sem.at[part])

    def output_store():
        return pltpu.make_async_copy(output_out, output, out_sem.at[0])

    def features_store():
        return pltpu.make_async_copy(features_out, grad_features, out_sem.at[1])

    def weight_store():
        return pltpu.make_async_copy(weight_out, grad_weight, out_sem.at[2])

    def bias_store():
        return pltpu.make_async_copy(bias_out, grad_bias, out_sem.at[3])

    mine = pltpu.make_async_copy(features, feat.at[pl.ds(row * N, N)], in_sem.at[3])
    mine.start()
    for part in range(LOADS):
        tile_load(part).start()
    for part in range(3):
        load(part).start()
    mine.wait()
    pl.semaphore_wait(barrier, len(partners))

    def feat_rows(yy, hh, half):
        return feat.at[pl.ds((yy * 2 + hh) * N + half * HALF, HALF)]

    def feat_across(half):
        here = feat_rows(y, h, half)
        return remote(here, here, fh_s.at[half], fh_r.at[half], across, col)

    def feat_across_in(half):
        there = feat_rows(y, 1 - h, half)
        return remote(there, there, fh_s.at[half], fh_r.at[half], across, col)

    def feat_y(kind, way, g):
        hh = h if g == 0 else 1 - h
        behind = (y + (3 if way == 0 else 1)) % 4
        block = feat_rows(behind if kind == 2 else y, hh, way if kind != 1 else 1 - way)
        return remote(block, block, fy_s.at[kind, way, g], fy_r.at[kind, way, g], y_next[way], col)

    def feat_y_in(kind, way, g):
        hh = h if g == 0 else 1 - h
        behind = (y + (3 if way == 0 else 1)) % 4
        source = (y + 2) % 4 if kind == 2 else behind
        block = feat_rows(source, hh, way if kind != 1 else 1 - way)
        return remote(block, block, fy_s.at[kind, way, g], fy_r.at[kind, way, g], y_next[way], col)

    for half in range(2):
        feat_across(half).start()
    for way in range(2):
        feat_y(0, way, 0).start()
    tiles[SLOTS] = jnp.zeros((TILE, TILE), BF16)
    acc[...] = jnp.zeros(acc.shape, F32)
    for way in range(2):
        feat_y(0, way, 0).wait_send()
    for way in range(2):
        feat_y(1, way, 0).start()
    for way in range(2):
        feat_y_in(0, way, 0).wait_recv()
        feat_y(2, way, 0).start()

    def fill(place, carry):
        slot = SLOTS
        for i in range(SLOTS):
            slot = jnp.where((located[i] == place) & (limit[0] > i), i, slot)
        slots[place] = slot
        return carry

    lax.fori_loop(0, 64, fill, 0)
    for way in range(2):
        feat_y_in(1, way, 0).wait_recv()
        feat_y_in(2, way, 0).wait_recv()
    for part in range(LOADS):
        tile_load(part).wait()

    def row_tile(s):
        xx = (x + pick(s % 4, [2, 1, 3, 0])) % 4
        return xx * 4 + order_far_first(s // 4, z)

    def forward_half(t, k_half, hh):
        total = None
        lanes = pl.ds(pl.multiple_of(hh * N, N), N)
        for c in range(4):
            part = jnp.dot(
                tiles[slots[t * 4 + c], pl.ds(pl.multiple_of(k_half * N, N), N), lanes],
                feat[pl.ds(pl.multiple_of((c * 2 + hh) * N, N), N), :],
                preferred_element_type=F32,
            )
            total = part if total is None else total + part
        return total

    def early_step(s, carry):
        @pl.when(s == EARLY)
        def _():
            for half in range(2):
                feat_across_in(half).wait_recv()
                feat_y(0, half, 1).start()

        @pl.when(s == EARLY + GAP)
        def _():
            for way in range(2):
                feat_y(1, way, 1).start()

        @pl.when(s == EARLY + GAP + 2)
        def _():
            for way in range(2):
                feat_y_in(0, way, 1).wait_recv()
                feat_y(2, way, 1).start()

        t = row_tile(s)
        part_sums[s, 0] = forward_half(t, other, h)
        part_sums[s, 1] = forward_half(t, k, h)
        return carry

    lax.fori_loop(0, 16, early_step, 0)
    for way in range(2):
        feat_y_in(1, way, 1).wait_recv()
        feat_y_in(2, way, 1).wait_recv()

    def pair_copy(u):
        return remote(pair_out.at[u], pair_in.at[u], pair_s.at[u], pair_r.at[u], row, twin)

    def x_copy(kind, way, j):
        if kind == 0:
            src, dst = xa.at[j, rows(way)], xra.at[way, j]
        elif kind == 1:
            src, dst = xb.at[way, j], xrb.at[way, j]
        else:
            src, dst = xc.at[way, j], xrc.at[way, j]
        return remote(src, dst, x_s.at[kind, way, j], x_r.at[kind, way, j], row, x_next[way])

    def z_copy(j):
        target = order_far_first(j, z)
        way = jnp.where(target > z, 0, 1)
        to = jnp.where(target > z, z_up, z_down)
        return remote(zs.at[j], zr.at[way, target], z_s.at[j], z_r.at[way, target], row, to)

    def z_wait(way, target):
        block = zr.at[way, target]
        remote(zs.at[0], block, z_s.at[0], z_r.at[way, target], row, twin).wait_recv()

    def relay(j):
        for way in range(2):
            x_copy(0, way, j).wait_recv()
            xc[way, j] = (part_sums[4 * j + 1 + way, 1, rows(way), :] + xra[way, j].astype(F32)).astype(BF16)
            x_copy(2, way, j).start()

    def collect(j):
        u = 4 * j + 3
        for way in range(2):
            x_copy(1, way, j).wait_recv()
            x_copy(2, way, j).wait_recv()
        for half in range(2):
            part_sums[u, 1, rows(half), :] = (
                part_sums[u, 1, rows(half), :] + xrc[half, j].astype(F32) + xrb[1 - half, j].astype(F32)
            )

        @pl.when(edge & (j < 3))
        def _():
            zs[j] = part_sums[u, 1].astype(BF16)
            z_copy(j).start()

        def middle(jj):
            target = order_far_first(jj, z)
            way = jnp.where(target > z, 0, 1)
            z_wait(way, target)
            zs[jj] = (part_sums[4 * jj + 3, 1] + zr[way, target].astype(F32)).astype(BF16)
            z_copy(jj).start()

        @pl.when(jnp.logical_not(edge) & (j == 1))
        def _():
            middle(0)

        @pl.when(jnp.logical_not(edge) & (j == 2))
        def _():
            middle(1)
            middle(2)

    def forward_step(s, carry):
        @pl.when(s < 16)
        def _():
            t = row_tile(s)
            pair_out[s] = (part_sums[s, 0] + forward_half(t, other, 1 - h)).astype(BF16)
            pair_copy(s).start()
            part_sums[s, 1] = part_sums[s, 1] + forward_half(t, k, 1 - h)

        @pl.when((s >= LAG) & (s < 16 + LAG))
        def _():
            u = s - LAG
            j = u // 4
            pair_copy(u).wait_recv()

            @pl.when(u % 4 == 0)
            def _():
                xa[j] = (part_sums[u, 1] + pair_in[u].astype(F32)).astype(BF16)
                x_copy(0, 0, j).start()
                x_copy(0, 1, j).start()

            for way in range(2):

                @pl.when(u % 4 == 1 + way)
                def _():
                    far, near = rows(way), rows(1 - way)
                    xb[way, j] = (part_sums[u, 1, near, :] + pair_in[u, near, :].astype(F32)).astype(BF16)
                    x_copy(1, way, j).start()
                    part_sums[u, 1, far, :] = part_sums[u, 1, far, :] + pair_in[u, far, :].astype(F32)

            @pl.when(u % 4 == 3)
            def _():
                part_sums[u, 1] = part_sums[u, 1] + pair_in[u].astype(F32)

        v = s - LAG - RV

        @pl.when((v >= 0) & (v < 16) & (v % 4 == 0))
        def _():
            relay(v // 4)

        w = s - LAG - CV

        @pl.when((w >= 0) & (w % 4 == 0))
        def _():
            collect(w // 4)

        return carry

    lax.fori_loop(0, LAG + CV + 13, forward_step, 0)

    @pl.when(z > 0)
    def _():
        z_wait(0, z)
        part_sums[15, 1] = part_sums[15, 1] + zr[0, z].astype(F32)

    @pl.when(z < 3)
    def _():
        z_wait(1, z)
        part_sums[15, 1] = part_sums[15, 1] + zr[1, z].astype(F32)

    gathered = part_sums[15, 1]
    for part in range(3):
        load(part).wait()
    shifted = split_dot(gathered, weight_in[...], (((1,), (0,)), ((), ()))) + bias_in[...]
    sigma = jax.nn.sigmoid(shifted)
    output_out[...] = (shifted * sigma).astype(BF16)
    output_store().start()
    signal = (cotangent_in[...].astype(F32) * (sigma * (1.0 + shifted * (1.0 - sigma)))).astype(BF16)
    work[...] = signal
    sig[x * 4 + z, k] = signal.astype(F32).T.astype(BF16)

    def sig_pair(t, kk):
        block = sig.at[t, kk]
        return remote(block, block, gp_s.at[t], gp_r.at[t], row, twin)

    def sig_z(way, piece):
        block = sig.at[x * 4 + piece, k]
        return remote(block, block, gz_s.at[way, piece], gz_r.at[way, piece], row, z_next[way])

    def sig_x(kind, way, j, arriving=False):
        piece = order_near_first(j, z)
        behind = (x + (3 if way == 0 else 1)) % 4
        if arriving:
            source = (x + 2) % 4 if kind == 2 else behind
        else:
            source = behind if kind == 2 else x
        block = sig.at[source * 4 + piece, k, rows(way if kind != 1 else 1 - way)]
        return remote(block, block, gx_s.at[kind, way, j], gx_r.at[kind, way, j], row, x_next[way])

    def launch_piece(j):
        for way in range(2):
            sig_x(0, way, j).start()
        sig_pair(x * 4 + order_near_first(j, z), k).start()

    for way in range(2):
        sig_x(0, way, 0).start()

    @pl.when(z < 3)
    def _():
        sig_z(0, z).start()

    @pl.when(z > 0)
    def _():
        sig_z(1, z).start()

    sig_pair(x * 4 + z, k).start()

    def wa_copy(to, here):
        return remote(wa.at[to], wra.at[here], wa_s.at[to], wa_r.at[here], to * 2 + h, col)

    def wk_copy():
        return remote(wb.at[other], wk, wk_s.at[0], wk_r.at[0], row, twin)

    def wx_copy(to, here):
        return remote(wc.at[to], wx.at[here], wx_s.at[to], wx_r.at[here], row, column(to, z, k))

    def wz_copy(to, here):
        return remote(
            wz.at[here], wz.at[here], wz_s.at[to], wz_r.at[here], y * 2 + to // 4, column(x, to % 4, k)
        )

    def wd_copy(to, here):
        return remote(wd.at[here], wd.at[here], wd_s.at[to], wd_r.at[here], row, column(to, z, k))

    def we_copy(here):
        return remote(we.at[here], we.at[here], we_s.at[0], we_r.at[0], row, twin)

    def wg_copy(to, here):
        return remote(wg.at[here], wg.at[here], wg_s.at[to], wg_r.at[here], to * 2 + h, col)

    def total_of(ref, count):
        total = ref[0]
        for place in range(1, count):
            total = total + ref[place]
        return total

    place8 = h * 4 + z

    part = split_dot(gathered.T, work[...], (((1,), (0,)), ((), ())))
    bias_part = jnp.sum(work[...].astype(F32), axis=0, keepdims=True)
    line = lax.broadcasted_iota(jnp.int32, (8, HALF), 0)
    bias_block = jnp.where(line == 0, jnp.broadcast_to(bias_part[:, 0:HALF], (8, HALF)), 0.0) + jnp.where(
        line == 1, jnp.broadcast_to(bias_part[:, HALF:N], (8, HALF)), 0.0
    )
    for piece in range(32):
        wa[piece // 8, piece // 4 % 2, piece % 4, :, 0:N] = part[piece * 8 : piece * 8 + 8, :]
        wa[piece // 8, piece // 4 % 2, piece % 4, :, N : N + HALF] = bias_block
    for way in range(2):
        sig_x(1, way, 0).start()
    for step in range(1, 4):
        wa_copy((y + step) % 4, y).start()
    wra[y] = wa[y]

    def weights_rows():
        for step in range(1, 4):
            wa_copy((y + step) % 4, (y + step) % 4).wait_recv()
        wb[...] = total_of(wra, 4)
        wk_copy().start()

    def weights_pair():
        wk_copy().wait_recv()
        wc[...] = wb[k] + wk[...]
        for step in range(1, 4):
            wx_copy((x + step) % 4, x).start()
        wx[x] = wc[x]

    def weights_x():
        for step in range(1, 4):
            wx_copy((x + step) % 4, (x + step) % 4).wait_recv()
        wz[place8] = total_of(wx, 4)
        for step in range(1, 8):
            wz_copy((place8 + step) % 8, place8).start()

    def weights_z():
        for step in range(1, 8):
            wz_copy((place8 + step) % 8, (place8 + step) % 8).wait_recv()
        total = total_of(wz, 8) * scale
        wd[x] = total[:, 0:N]
        bias_out[0:1, 0:HALF] = total[0:1, N : N + HALF]
        bias_out[0:1, HALF:N] = total[1:2, N : N + HALF]
        bias_store().start()
        for step in range(1, 4):
            wd_copy((x + step) % 4, x).start()

    def weights_back():
        for step in range(1, 4):
            wd_copy((x + step) % 4, (x + step) % 4).wait_recv()
        we[k] = wd[...]
        we_copy(k).start()

    def weights_twin():
        we_copy(other).wait_recv()
        wg[y] = we[...]
        for step in range(1, 4):
            wg_copy((y + step) % 4, y).start()

    def weights_end():
        for step in range(1, 4):
            wg_copy((y + step) % 4, (y + step) % 4).wait_recv()
        for piece in range(32):
            weight_out[piece * 8 : piece * 8 + 8, :] = wg[piece // 8, piece // 4 % 2, piece % 4]
        weight_store().start()

    def relay_signal(j):
        for way in range(2):
            sig_x(0, way, j, True).wait_recv()
            sig_x(2, way, j).start()

    def next_piece(jj):
        piece = order_near_first(jj, z)

        @pl.when(z == 0)
        def _():
            sig_z(1, piece).wait_recv()

        @pl.when(z == 3)
        def _():
            sig_z(0, piece).wait_recv()

        @pl.when(jnp.logical_not(edge) & (jj == 1))
        def _():
            sig_z(0, z - 1).wait_recv()
            sig_z(0, z - 1).start()
            sig_z(1, z + 1).wait_recv()
            sig_z(1, z + 1).start()

        @pl.when((z == 1) & (jj == 2))
        def _():
            sig_z(1, 3).wait_recv()
            sig_z(1, 3).start()

        @pl.when((z == 2) & (jj == 2))
        def _():
            sig_z(0, 0).wait_recv()
            sig_z(0, 0).start()

        launch_piece(jj)

    def backward_step(s, carry):
        j = s // 4

        @pl.when(s == 0)
        def _():
            relay_signal(0)
            next_piece(1)

        @pl.when((s == 4) | (s == 8))
        def _():
            next_piece(j + 1)

        @pl.when((s % 4 == 0) & (s >= 4) & (s < 16))
        def _():
            relay_signal(j)

        @pl.when((s % 4 == 0) & (s >= 4))
        def _():
            for way in range(2):
                sig_x(2, way, j - 1, True).wait_recv()
            sig_pair(((x + 2) % 4) * 4 + order_near_first(j - 1, z), k).start()

        @pl.when((s % 4 == 1) & (s < 16))
        def _():
            piece = order_near_first(j, z)
            for way in range(2):
                sig_x(1, way, j, True).wait_recv()
                sig_pair(((x + (3 if way == 0 else 1)) % 4) * 4 + piece, k).start()

        @pl.when((s == 2) | (s == 6) | (s == 10))
        def _():
            for way in range(2):
                sig_x(1, way, s // 4 + 1).start()

        for when, what in (
            (HA, weights_rows), (HB, weights_pair), (HC, weights_x), (HD, weights_z), (HE, weights_back),
        ):

            @pl.when(s == when)
            def _(what=what):
                what()

        last = s % 4 == 1

        @pl.when((s != 1) & (s != 16))
        def _():
            jj = jnp.where(last, j - 1, j)
            shift = pick(s % 4, [0, 2, 3, 1])
            t = ((x + shift) % 4) * 4 + order_near_first(jj, z)
            sig_pair(t, other).wait_recv()
            for c in range(4):
                slot = slots[t * 4 + c]
                part = jnp.dot(sig[t, 0], tiles[slot, 0:N, :], preferred_element_type=F32) + jnp.dot(
                    sig[t, 1], tiles[slot, N:TILE, :], preferred_element_type=F32
                )
                acc[c, 0] += part[:, 0:N]
                acc[c, 1] += part[:, N:TILE]

        return carry

    lax.fori_loop(0, 18, backward_step, 0)

    def y_copy(kind, way, g):
        if kind == 0:
            src, dst = ya.at[g, rows(way)], yra.at[way, g]
        elif kind == 1:
            src, dst = yb.at[way, g], yrb.at[way, g]
        else:
            src, dst = yc.at[way, g], yrc.at[way, g]
        return remote(src, dst, y_s.at[kind, way, g], y_r.at[kind, way, g], y_next[way], col)

    def y_open(g):
        hh = 1 - h if g == 0 else h
        ya[g] = acc[(y + 2) % 4, hh].astype(BF16)
        for way in range(2):
            y_copy(0, way, g).start()
        for way in range(2):
            yb[way, g] = acc[(y + (1 if way == 0 else 3)) % 4, hh, rows(1 - way), :].astype(BF16)
            y_copy(1, way, g).start()

    def y_relay(g):
        hh = 1 - h if g == 0 else h
        for way in range(2):
            y_copy(0, way, g).wait_recv()
            near = acc[(y + (1 if way == 0 else 3)) % 4, hh, rows(way), :]
            yc[way, g] = (near + yra[way, g].astype(F32)).astype(BF16)
            y_copy(2, way, g).start()

    def y_close(g):
        hh = 1 - h if g == 0 else h
        for way in range(2):
            y_copy(1, way, g).wait_recv()
            y_copy(2, way, g).wait_recv()
        for half in range(2):
            acc[y, hh, rows(half), :] = (
                acc[y, hh, rows(half), :] + yrc[half, g].astype(F32) + yrb[1 - half, g].astype(F32)
            )

    def q_copy(half):
        return remote(qs.at[half], qr.at[half], q_s.at[half], q_r.at[half], across, col)

    def sent():
        for half in range(2):
            feat_across(half).wait_send()
        for kind in range(3):
            for way in range(2):
                for g in range(2):
                    if (kind, g) != (0, 0):
                        feat_y(kind, way, g).wait_send()

        def sent_pair(u, carry):
            pair_copy(u).wait_send()
            sig_pair(u, k).wait_send()
            return carry

        lax.fori_loop(0, 16, sent_pair, 0)

        def sent_x(j, carry):
            for kind in range(3):
                for way in range(2):
                    x_copy(kind, way, j).wait_send()
                    sig_x(kind, way, j).wait_send()
            return carry

        lax.fori_loop(0, 4, sent_x, 0)
        for j in range(3):
            z_copy(j).wait_send()
        for piece in range(4):

            @pl.when((z < 3) & (piece <= z))
            def _():
                sig_z(0, piece).wait_send()

            @pl.when((z > 0) & (piece >= z))
            def _():
                sig_z(1, piece).wait_send()

        for step in range(1, 4):
            wa_copy((y + step) % 4, y).wait_send()
            wx_copy((x + step) % 4, x).wait_send()
            wd_copy((x + step) % 4, x).wait_send()
        for step in range(1, 8):
            wz_copy((place8 + step) % 8, place8).wait_send()
        wk_copy().wait_send()
        we_copy(k).wait_send()

    y_open(0)
    y_relay(0)
    y_open(1)
    weights_twin()
    y_close(0)
    for half in range(2):
        qs[half] = acc[y, 1 - h, rows(half), :].astype(BF16)
        q_copy(half).start()
    y_relay(1)
    y_close(1)
    weights_end()
    sent()
    for kind in range(3):
        for way in range(2):
            for g in range(2):
                y_copy(kind, way, g).wait_send()
    for step in range(1, 4):
        wg_copy((y + step) % 4, y).wait_send()
    output_store().wait()
    weight_store().wait()
    bias_store().wait()
    for half in range(2):
        q_copy(half).wait_recv()
        acc[y, h, rows(half), :] = acc[y, h, rows(half), :] + qr[half].astype(F32)
    features_out[...] = split_dot(acc[y, h].T, weight_in[...], (((1,), (1,)), ((), ()))).astype(BF16)
    features_store().start()


    for half in range(2):
        q_copy(half).wait_send()
    features_store().wait()


def hand_over(output, grad_features, grad_weight, grad_bias, output_to, features_to, weight_to, bias_to):
    output_to[...] = output[...]
    features_to[...] = grad_features[...]
    weight_to[...] = grad_weight[...]
    bias_to[...] = grad_bias[...]


def on_device(features, weight, bias_vector, adjacency_tiles, tile_index, tile_count, grad_output):
    vmem = pl.BlockSpec(memory_space=pltpu.VMEM)
    scalars = pl.BlockSpec(memory_space=pltpu.SMEM)
    anywhere = pl.BlockSpec(memory_space=pl.ANY)
    dma = pltpu.SemaphoreType.DMA
    output, grad_features, grad_weight, grad_bias = pl.pallas_call(
        kernel,
        out_shape=(
            jax.ShapeDtypeStruct((N, N), BF16),
            jax.ShapeDtypeStruct((N, N), BF16),
            jax.ShapeDtypeStruct((N, N), F32),
            jax.ShapeDtypeStruct((1, N), F32),
        ),
        in_specs=[
            scalars, scalars, anywhere, anywhere, anywhere, anywhere, anywhere,
        ],
        out_specs=(anywhere, anywhere, anywhere, anywhere),
        scratch_shapes=[
            pltpu.VMEM((SLOTS + 1, TILE, TILE), BF16),
            pltpu.VMEM((8 * N, N), BF16),
            pltpu.VMEM((16, N, N), BF16),
            pltpu.VMEM((16, N, N), BF16),
            pltpu.VMEM((4, N, N), BF16),
            pltpu.VMEM((2, 4, HALF, N), BF16),
            pltpu.VMEM((2, 4, HALF, N), BF16),
            pltpu.VMEM((2, 4, HALF, N), BF16),
            pltpu.VMEM((2, 4, HALF, N), BF16),
            pltpu.VMEM((2, 4, HALF, N), BF16),
            pltpu.VMEM((3, N, N), BF16),
            pltpu.VMEM((2, 4, N, N), BF16),
            pltpu.VMEM((16, 2, N, N), BF16),
            pltpu.VMEM((4, 2, N, N), F32),
            pltpu.VMEM((2, N, N), BF16),
            pltpu.VMEM((2, 2, HALF, N), BF16),
            pltpu.VMEM((2, 2, HALF, N), BF16),
            pltpu.VMEM((2, 2, HALF, N), BF16),
            pltpu.VMEM((2, 2, HALF, N), BF16),
            pltpu.VMEM((2, 2, HALF, N), BF16),
            pltpu.VMEM((2, HALF, N), BF16),
            pltpu.VMEM((2, HALF, N), BF16),
            pltpu.VMEM((4, 2, 4, 8, N + HALF), F32),
            pltpu.VMEM((4, 2, 4, 8, N + HALF), F32),
            pltpu.VMEM((2, 4, 8, N + HALF), F32),
            pltpu.VMEM((4, 8, N + HALF), F32),
            pltpu.VMEM((4, 8, N + HALF), F32),
            pltpu.VMEM((4, 8, N + HALF), F32),
            pltpu.VMEM((8, 8, N + HALF), F32),
            pltpu.VMEM((4, 8, N), F32),
            pltpu.VMEM((2, 4, 8, N), F32),
            pltpu.VMEM((4, 2, 4, 8, N), F32),
            pltpu.VMEM((N, N), BF16),
            pltpu.VMEM((16, 2, N, N), F32),
            pltpu.VMEM((N, N), BF16),
            pltpu.VMEM((1, N), F32),
            pltpu.VMEM((N, N), BF16),
            pltpu.VMEM((N, N), BF16),
            pltpu.VMEM((N, N), BF16),
            pltpu.VMEM((N, N), F32),
            pltpu.VMEM((1, N), F32),
            dma((LOADS,)),
            dma((3, 2, 2)), dma((3, 2, 2)), dma((2,)), dma((2,)),
            dma((16,)), dma((16,)), dma((3, 2, 4)), dma((3, 2, 4)), dma((3,)), dma((2, 4)),
            dma((16,)), dma((16,)), dma((3, 2, 4)), dma((3, 2, 4)), dma((2, 4)), dma((2, 4)),
            dma((3, 2, 2)), dma((3, 2, 2)), dma((2,)), dma((2,)),
            dma((4,)), dma((4,)), dma((1,)), dma((1,)), dma((4,)), dma((4,)), dma((8,)), dma((8,)),
            dma((4,)), dma((4,)), dma((1,)), dma((1,)), dma((4,)), dma((4,)), dma((4,)), dma((4,)),
            pltpu.SMEM((64,), jnp.int32),
        ],
        compiler_params=pltpu.CompilerParams(
            collective_id=0, has_side_effects=True, vmem_limit_bytes=56 * 1024 * 1024
        ),
        name="graph_layer",
    )(tile_index[0, 0], tile_count[0], features, weight, bias_vector[None, :], adjacency_tiles[0, 0], grad_output)
    output, grad_features, grad_weight, grad_bias = pl.pallas_call(
        hand_over,
        out_shape=(
            jax.ShapeDtypeStruct((N, N), BF16),
            jax.ShapeDtypeStruct((N, N), BF16),
            jax.ShapeDtypeStruct((N, N), F32),
            jax.ShapeDtypeStruct((1, N), F32),
        ),
        in_specs=[vmem, vmem, vmem, vmem],
        out_specs=(vmem, vmem, vmem, vmem),
        name="hand_over",
    )(output, grad_features, grad_weight, grad_bias)
    return output, grad_features, grad_weight, grad_bias[0]


def solution(mesh):
    return jax.shard_map(
        on_device,
        mesh=mesh,
        in_specs=(
            P(("col", "row"), None),
            P(),
            P(),
            P("row", "col", None, None, None),
            P("row", "col", None),
            P("row", "col"),
            P(("row", "col"), None),
        ),
        out_specs=(P(("row", "col"), None), P(("col", "row"), None), P(), P()),
        check_vma=False,
    )
```

```python
import math

import jax
import jax.numpy as jnp
from jax import lax
from jax.experimental import pallas as pl
from jax.experimental.pallas import tpu as pltpu
from jax.sharding import PartitionSpec as P

MESH = pl.DeviceIdType.MESH
F32 = jnp.float32
BF16 = jnp.bfloat16
N = 256
HALF = 128
TILE = 512
SLOTS = 24
LOADS = 8
LAG = 2
EARLY = 4
GAP = 3
HA = 2
HB = 5
HC = 9
HD = 13
HE = 17
RV = 3
CV = 6


def pick(index, options):
    value = options[-1]
    for place in range(len(options) - 2, -1, -1):
        value = jnp.where(index == place, options[place], value)
    return value


def order_far_first(j, z):
    low = jnp.where(z < 2, z, 3 - z)
    base = jnp.where(low == 0, 3 - j, pick(j, [3, 0, 2, 1]))
    return jnp.where(z < 2, base, 3 - base)


def order_near_first(j, z):
    low = jnp.where(z < 2, z, 3 - z)
    base = jnp.where(low == 0, j, pick(j, [1, 0, 2, 3]))
    return jnp.where(z < 2, base, 3 - base)


def split_dot(left, right, dims):
    high = left.astype(BF16)
    low = (left - high.astype(F32)).astype(BF16)
    return lax.dot_general(high, right, dims, preferred_element_type=F32) + lax.dot_general(
        low, right, dims, preferred_element_type=F32
    )


def kernel(
    located, limit, features, weight, bias, tiles_hbm, cotangent,
    output, grad_features, grad_weight, grad_bias,
    tiles, feat, pair_out, pair_in, xa, xb, xc, xra, xrb, xrc, zs, zr,
    sig, acc, ya, yb, yc, yra, yrb, yrc, qs, qr,
    wa, wra, wb, wk, wc, wx, wz, wd, we, wg, work, part_sums,
    weight_in, bias_in, cotangent_in, output_out, features_out, weight_out, bias_out,
    load_sem, fy_s, fy_r, fh_s, fh_r, pair_s, pair_r, x_s, x_r, z_s, z_r,
    gp_s, gp_r, gx_s, gx_r, gz_s, gz_r, y_s, y_r, q_s, q_r,
    wa_s, wa_r, wk_s, wk_r, wx_s, wx_r, wz_s, wz_r, wd_s, wd_r, we_s, we_r, wg_s, wg_r, in_sem, out_sem, slots,
):
    row, col = lax.axis_index("row"), lax.axis_index("col")
    y, h = row // 2, row % 2
    x, z, k = col // 8, (col // 2) % 4, col % 2
    other = 1 - k
    scale = 1.0 / math.sqrt(65536)

    def column(xx, zz, kk):
        return (xx * 4 + zz) * 2 + kk

    def remote(src, dst, send, recv, to_row, to_col):
        return pltpu.make_async_remote_copy(
            src_ref=src, dst_ref=dst, send_sem=send, recv_sem=recv,
            device_id=(to_row, to_col), device_id_type=MESH,
        )

    x_next = [column((x + 1) % 4, z, k), column((x + 3) % 4, z, k)]
    y_next = [((y + 1) % 4) * 2 + h, ((y + 3) % 4) * 2 + h]
    z_up = column(x, jnp.minimum(z + 1, 3), k)
    z_down = column(x, jnp.maximum(z - 1, 0), k)
    z_next = [z_up, z_down]
    twin = column(x, z, other)
    across = y * 2 + 1 - h
    edge = (z == 0) | (z == 3)

    def rows(half):
        return pl.ds(half * HALF, HALF)

    barrier = pltpu.get_barrier_semaphore()
    partners = [(row, twin)]
    for step in range(1, 4):
        partners.append((row, column((x + step) % 4, z, k)))
        partners.append((((y + step) % 4) * 2 + h, col))
    for step in range(1, 8):
        place = (h * 4 + z + step) % 8
        partners.append((y * 2 + place // 4, column(x, place % 4, k)))
    for to_row, to_col in partners:
        pl.semaphore_signal(barrier, inc=1, device_id=(to_row, to_col), device_id_type=MESH)

    def tile_load(part):
        count = SLOTS // LOADS
        return pltpu.make_async_copy(
            tiles_hbm.at[pl.ds(part * count, count)], tiles.at[pl.ds(part * count, count)], load_sem.at[part]
        )

    def load(part):
        src, dst = ((weight, weight_in), (bias, bias_in), (cotangent, cotangent_in))[part]
        return pltpu.make_async_copy(src, dst, in_sem.at[part])

    def output_store():
        return pltpu.make_async_copy(output_out, output, out_sem.at[0])

    def features_store():
        return pltpu.make_async_copy(features_out, grad_features, out_sem.at[1])

    def weight_store():
        return pltpu.make_async_copy(weight_out, grad_weight, out_sem.at[2])

    def bias_store():
        return pltpu.make_async_copy(bias_out, grad_bias, out_sem.at[3])

    mine = pltpu.make_async_copy(features, feat.at[pl.ds(row * N, N)], in_sem.at[3])
    mine.start()
    for part in range(LOADS):
        tile_load(part).start()
    for part in range(3):
        load(part).start()
    mine.wait()
    pl.semaphore_wait(barrier, len(partners))

    def feat_rows(yy, hh, half):
        return feat.at[pl.ds((yy * 2 + hh) * N + half * HALF, HALF)]

    def feat_across(half):
        here = feat_rows(y, h, half)
        return remote(here, here, fh_s.at[half], fh_r.at[half], across, col)

    def feat_across_in(half):
        there = feat_rows(y, 1 - h, half)
        return remote(there, there, fh_s.at[half], fh_r.at[half], across, col)

    def feat_y(kind, way, g):
        hh = h if g == 0 else 1 - h
        behind = (y + (3 if way == 0 else 1)) % 4
        block = feat_rows(behind if kind == 2 else y, hh, way if kind != 1 else 1 - way)
        return remote(block, block, fy_s.at[kind, way, g], fy_r.at[kind, way, g], y_next[way], col)

    def feat_y_in(kind, way, g):
        hh = h if g == 0 else 1 - h
        behind = (y + (3 if way == 0 else 1)) % 4
        source = (y + 2) % 4 if kind == 2 else behind
        block = feat_rows(source, hh, way if kind != 1 else 1 - way)
        return remote(block, block, fy_s.at[kind, way, g], fy_r.at[kind, way, g], y_next[way], col)

    for half in range(2):
        feat_across(half).start()
    for way in range(2):
        feat_y(0, way, 0).start()
    tiles[SLOTS] = jnp.zeros((TILE, TILE), BF16)
    acc[...] = jnp.zeros(acc.shape, F32)
    for way in range(2):
        feat_y(0, way, 0).wait_send()
    for way in range(2):
        feat_y(1, way, 0).start()
    for way in range(2):
        feat_y_in(0, way, 0).wait_recv()
        feat_y(2, way, 0).start()

    def fill(place, carry):
        slot = SLOTS
        for i in range(SLOTS):
            slot = jnp.where((located[i] == place) & (limit[0] > i), i, slot)
        slots[place] = slot
        return carry

    lax.fori_loop(0, 64, fill, 0)
    for way in range(2):
        feat_y_in(1, way, 0).wait_recv()
        feat_y_in(2, way, 0).wait_recv()
    for part in range(LOADS):
        tile_load(part).wait()

    def row_tile(s):
        xx = (x + pick(s % 4, [2, 1, 3, 0])) % 4
        return xx * 4 + order_far_first(s // 4, z)

    def forward_half(t, k_half, hh):
        total = None
        lanes = pl.ds(pl.multiple_of(hh * N, N), N)
        for c in range(4):
            part = jnp.dot(
                tiles[slots[t * 4 + c], pl.ds(pl.multiple_of(k_half * N, N), N), lanes],
                feat[pl.ds(pl.multiple_of((c * 2 + hh) * N, N), N), :],
                preferred_element_type=F32,
            )
            total = part if total is None else total + part
        return total

    def early_step(s, carry):
        @pl.when(s == EARLY)
        def _():
            for half in range(2):
                feat_across_in(half).wait_recv()
                feat_y(0, half, 1).start()

        @pl.when(s == EARLY + GAP)
        def _():
            for way in range(2):
                feat_y(1, way, 1).start()

        @pl.when(s == EARLY + GAP + 2)
        def _():
            for way in range(2):
                feat_y_in(0, way, 1).wait_recv()
                feat_y(2, way, 1).start()

        t = row_tile(s)
        part_sums[s, 0] = forward_half(t, other, h)
        part_sums[s, 1] = forward_half(t, k, h)
        return carry

    lax.fori_loop(0, 16, early_step, 0)
    for way in range(2):
        feat_y_in(1, way, 1).wait_recv()
        feat_y_in(2, way, 1).wait_recv()

    def pair_copy(u):
        return remote(pair_out.at[u], pair_in.at[u], pair_s.at[u], pair_r.at[u], row, twin)

    def x_copy(kind, way, j):
        if kind == 0:
            src, dst = xa.at[j, rows(way)], xra.at[way, j]
        elif kind == 1:
            src, dst = xb.at[way, j], xrb.at[way, j]
        else:
            src, dst = xc.at[way, j], xrc.at[way, j]
        return remote(src, dst, x_s.at[kind, way, j], x_r.at[kind, way, j], row, x_next[way])

    def z_copy(j):
        target = order_far_first(j, z)
        way = jnp.where(target > z, 0, 1)
        to = jnp.where(target > z, z_up, z_down)
        return remote(zs.at[j], zr.at[way, target], z_s.at[j], z_r.at[way, target], row, to)

    def z_wait(way, target):
        block = zr.at[way, target]
        remote(zs.at[0], block, z_s.at[0], z_r.at[way, target], row, twin).wait_recv()

    def relay(j):
        for way in range(2):
            x_copy(0, way, j).wait_recv()
            xc[way, j] = (part_sums[4 * j + 1 + way, 1, rows(way), :] + xra[way, j].astype(F32)).astype(BF16)
            x_copy(2, way, j).start()

    def collect(j):
        u = 4 * j + 3
        for way in range(2):
            x_copy(1, way, j).wait_recv()
            x_copy(2, way, j).wait_recv()
        for half in range(2):
            part_sums[u, 1, rows(half), :] = (
                part_sums[u, 1, rows(half), :] + xrc[half, j].astype(F32) + xrb[1 - half, j].astype(F32)
            )

        @pl.when(edge & (j < 3))
        def _():
            zs[j] = part_sums[u, 1].astype(BF16)
            z_copy(j).start()

        def middle(jj):
            target = order_far_first(jj, z)
            way = jnp.where(target > z, 0, 1)
            z_wait(way, target)
            zs[jj] = (part_sums[4 * jj + 3, 1] + zr[way, target].astype(F32)).astype(BF16)
            z_copy(jj).start()

        @pl.when(jnp.logical_not(edge) & (j == 1))
        def _():
            middle(0)

        @pl.when(jnp.logical_not(edge) & (j == 2))
        def _():
            middle(1)
            middle(2)

    def forward_step(s, carry):
        @pl.when(s < 16)
        def _():
            t = row_tile(s)
            pair_out[s] = (part_sums[s, 0] + forward_half(t, other, 1 - h)).astype(BF16)
            pair_copy(s).start()
            part_sums[s, 1] = part_sums[s, 1] + forward_half(t, k, 1 - h)

        @pl.when((s >= LAG) & (s < 16 + LAG))
        def _():
            u = s - LAG
            j = u // 4
            pair_copy(u).wait_recv()

            @pl.when(u % 4 == 0)
            def _():
                xa[j] = (part_sums[u, 1] + pair_in[u].astype(F32)).astype(BF16)
                x_copy(0, 0, j).start()
                x_copy(0, 1, j).start()

            for way in range(2):

                @pl.when(u % 4 == 1 + way)
                def _():
                    far, near = rows(way), rows(1 - way)
                    xb[way, j] = (part_sums[u, 1, near, :] + pair_in[u, near, :].astype(F32)).astype(BF16)
                    x_copy(1, way, j).start()
                    part_sums[u, 1, far, :] = part_sums[u, 1, far, :] + pair_in[u, far, :].astype(F32)

            @pl.when(u % 4 == 3)
            def _():
                part_sums[u, 1] = part_sums[u, 1] + pair_in[u].astype(F32)

        v = s - LAG - RV

        @pl.when((v >= 0) & (v < 16) & (v % 4 == 0))
        def _():
            relay(v // 4)

        w = s - LAG - CV

        @pl.when((w >= 0) & (w % 4 == 0))
        def _():
            collect(w // 4)

        return carry

    lax.fori_loop(0, LAG + CV + 13, forward_step, 0)

    @pl.when(z > 0)
    def _():
        z_wait(0, z)
        part_sums[15, 1] = part_sums[15, 1] + zr[0, z].astype(F32)

    @pl.when(z < 3)
    def _():
        z_wait(1, z)
        part_sums[15, 1] = part_sums[15, 1] + zr[1, z].astype(F32)

    gathered = part_sums[15, 1]
    for part in range(3):
        load(part).wait()
    shifted = split_dot(gathered, weight_in[...], (((1,), (0,)), ((), ()))) + bias_in[...]
    sigma = jax.nn.sigmoid(shifted)
    signal = (cotangent_in[...].astype(F32) * (sigma * (1.0 + shifted * (1.0 - sigma)))).astype(BF16)
    work[...] = signal
    sig[x * 4 + z, k] = signal.astype(F32).T.astype(BF16)

    def sig_pair(t, kk):
        block = sig.at[t, kk]
        return remote(block, block, gp_s.at[t], gp_r.at[t], row, twin)

    def sig_z(way, piece):
        block = sig.at[x * 4 + piece, k]
        return remote(block, block, gz_s.at[way, piece], gz_r.at[way, piece], row, z_next[way])

    def sig_x(kind, way, j, arriving=False):
        piece = order_near_first(j, z)
        behind = (x + (3 if way == 0 else 1)) % 4
        if arriving:
            source = (x + 2) % 4 if kind == 2 else behind
        else:
            source = behind if kind == 2 else x
        block = sig.at[source * 4 + piece, k, rows(way if kind != 1 else 1 - way)]
        return remote(block, block, gx_s.at[kind, way, j], gx_r.at[kind, way, j], row, x_next[way])

    def launch_piece(j):
        for way in range(2):
            sig_x(0, way, j).start()
        sig_pair(x * 4 + order_near_first(j, z), k).start()

    for way in range(2):
        sig_x(0, way, 0).start()

    @pl.when(z < 3)
    def _():
        sig_z(0, z).start()

    @pl.when(z > 0)
    def _():
        sig_z(1, z).start()

    sig_pair(x * 4 + z, k).start()
    output_out[...] = (shifted * sigma).astype(BF16)
    output_store().start()

    def wa_copy(to, here):
        return remote(wa.at[to], wra.at[here], wa_s.at[to], wa_r.at[here], to * 2 + h, col)

    def wk_copy():
        return remote(wb.at[other], wk, wk_s.at[0], wk_r.at[0], row, twin)

    def wx_copy(to, here):
        return remote(wc.at[to], wx.at[here], wx_s.at[to], wx_r.at[here], row, column(to, z, k))

    def wz_copy(to, here):
        return remote(
            wz.at[here], wz.at[here], wz_s.at[to], wz_r.at[here], y * 2 + to // 4, column(x, to % 4, k)
        )

    def wd_copy(to, here):
        return remote(wd.at[here], wd.at[here], wd_s.at[to], wd_r.at[here], row, column(to, z, k))

    def we_copy(here):
        return remote(we.at[here], we.at[here], we_s.at[0], we_r.at[0], row, twin)

    def wg_copy(to, here):
        return remote(wg.at[here], wg.at[here], wg_s.at[to], wg_r.at[here], to * 2 + h, col)

    def total_of(ref, count):
        total = ref[0]
        for place in range(1, count):
            total = total + ref[place]
        return total

    place8 = h * 4 + z

    part = split_dot(gathered.T, work[...], (((1,), (0,)), ((), ())))
    bias_part = jnp.sum(work[...].astype(F32), axis=0, keepdims=True)
    line = lax.broadcasted_iota(jnp.int32, (8, HALF), 0)
    bias_block = jnp.where(line == 0, jnp.broadcast_to(bias_part[:, 0:HALF], (8, HALF)), 0.0) + jnp.where(
        line == 1, jnp.broadcast_to(bias_part[:, HALF:N], (8, HALF)), 0.0
    )
    for piece in range(32):
        wa[piece // 8, piece // 4 % 2, piece % 4, :, 0:N] = part[piece * 8 : piece * 8 + 8, :]
        wa[piece // 8, piece // 4 % 2, piece % 4, :, N : N + HALF] = bias_block
    for way in range(2):
        sig_x(1, way, 0).start()
    for step in range(1, 4):
        wa_copy((y + step) % 4, y).start()
    wra[y] = wa[y]

    def weights_rows():
        for step in range(1, 4):
            wa_copy((y + step) % 4, (y + step) % 4).wait_recv()
        wb[...] = total_of(wra, 4)
        wk_copy().start()

    def weights_pair():
        wk_copy().wait_recv()
        wc[...] = wb[k] + wk[...]
        for step in range(1, 4):
            wx_copy((x + step) % 4, x).start()
        wx[x] = wc[x]

    def weights_x():
        for step in range(1, 4):
            wx_copy((x + step) % 4, (x + step) % 4).wait_recv()
        wz[place8] = total_of(wx, 4)
        for step in range(1, 8):
            wz_copy((place8 + step) % 8, place8).start()

    def weights_z():
        for step in range(1, 8):
            wz_copy((place8 + step) % 8, (place8 + step) % 8).wait_recv()
        total = total_of(wz, 8) * scale
        wd[x] = total[:, 0:N]
        bias_out[0:1, 0:HALF] = total[0:1, N : N + HALF]
        bias_out[0:1, HALF:N] = total[1:2, N : N + HALF]
        bias_store().start()
        for step in range(1, 4):
            wd_copy((x + step) % 4, x).start()

    def weights_back():
        for step in range(1, 4):
            wd_copy((x + step) % 4, (x + step) % 4).wait_recv()
        we[k] = wd[...]
        we_copy(k).start()

    def weights_twin():
        we_copy(other).wait_recv()
        wg[y] = we[...]
        for step in range(1, 4):
            wg_copy((y + step) % 4, y).start()

    def weights_end():
        for step in range(1, 4):
            wg_copy((y + step) % 4, (y + step) % 4).wait_recv()
        for piece in range(32):
            weight_out[piece * 8 : piece * 8 + 8, :] = wg[piece // 8, piece // 4 % 2, piece % 4]
        weight_store().start()

    def relay_signal(j):
        for way in range(2):
            sig_x(0, way, j, True).wait_recv()
            sig_x(2, way, j).start()

    def next_piece(jj):
        piece = order_near_first(jj, z)

        @pl.when(z == 0)
        def _():
            sig_z(1, piece).wait_recv()

        @pl.when(z == 3)
        def _():
            sig_z(0, piece).wait_recv()

        @pl.when(jnp.logical_not(edge) & (jj == 1))
        def _():
            sig_z(0, z - 1).wait_recv()
            sig_z(0, z - 1).start()
            sig_z(1, z + 1).wait_recv()
            sig_z(1, z + 1).start()

        @pl.when((z == 1) & (jj == 2))
        def _():
            sig_z(1, 3).wait_recv()
            sig_z(1, 3).start()

        @pl.when((z == 2) & (jj == 2))
        def _():
            sig_z(0, 0).wait_recv()
            sig_z(0, 0).start()

        launch_piece(jj)

    def backward_step(s, carry):
        j = s // 4

        @pl.when(s == 0)
        def _():
            relay_signal(0)
            next_piece(1)

        @pl.when((s == 4) | (s == 8))
        def _():
            next_piece(j + 1)

        @pl.when((s % 4 == 0) & (s >= 4) & (s < 16))
        def _():
            relay_signal(j)

        @pl.when((s % 4 == 0) & (s >= 4))
        def _():
            for way in range(2):
                sig_x(2, way, j - 1, True).wait_recv()
            sig_pair(((x + 2) % 4) * 4 + order_near_first(j - 1, z), k).start()

        @pl.when((s % 4 == 1) & (s < 16))
        def _():
            piece = order_near_first(j, z)
            for way in range(2):
                sig_x(1, way, j, True).wait_recv()
                sig_pair(((x + (3 if way == 0 else 1)) % 4) * 4 + piece, k).start()

        @pl.when((s == 2) | (s == 6) | (s == 10))
        def _():
            for way in range(2):
                sig_x(1, way, s // 4 + 1).start()

        for when, what in (
            (HA, weights_rows), (HB, weights_pair), (HC, weights_x), (HD, weights_z), (HE, weights_back),
        ):

            @pl.when(s == when)
            def _(what=what):
                what()

        last = s % 4 == 1

        @pl.when((s != 1) & (s != 16))
        def _():
            jj = jnp.where(last, j - 1, j)
            shift = pick(s % 4, [0, 2, 3, 1])
            t = ((x + shift) % 4) * 4 + order_near_first(jj, z)
            sig_pair(t, other).wait_recv()
            both = jnp.concatenate([sig[t, 0], sig[t, 1]], axis=1)
            for c in range(4):
                slot = slots[t * 4 + c]
                part = jnp.dot(both, tiles[slot], preferred_element_type=F32)
                acc[c, 0] += part[:, 0:N]
                acc[c, 1] += part[:, N:TILE]

        return carry

    lax.fori_loop(0, 18, backward_step, 0)

    def y_copy(kind, way, g):
        if kind == 0:
            src, dst = ya.at[g, rows(way)], yra.at[way, g]
        elif kind == 1:
            src, dst = yb.at[way, g], yrb.at[way, g]
        else:
            src, dst = yc.at[way, g], yrc.at[way, g]
        return remote(src, dst, y_s.at[kind, way, g], y_r.at[kind, way, g], y_next[way], col)

    def y_open(g):
        hh = 1 - h if g == 0 else h
        ya[g] = acc[(y + 2) % 4, hh].astype(BF16)
        for way in range(2):
            y_copy(0, way, g).start()
        for way in range(2):
            yb[way, g] = acc[(y + (1 if way == 0 else 3)) % 4, hh, rows(1 - way), :].astype(BF16)
            y_copy(1, way, g).start()

    def y_relay(g):
        hh = 1 - h if g == 0 else h
        for way in range(2):
            y_copy(0, way, g).wait_recv()
            near = acc[(y + (1 if way == 0 else 3)) % 4, hh, rows(way), :]
            yc[way, g] = (near + yra[way, g].astype(F32)).astype(BF16)
            y_copy(2, way, g).start()

    def y_close(g):
        hh = 1 - h if g == 0 else h
        for way in range(2):
            y_copy(1, way, g).wait_recv()
            y_copy(2, way, g).wait_recv()
        for half in range(2):
            acc[y, hh, rows(half), :] = (
                acc[y, hh, rows(half), :] + yrc[half, g].astype(F32) + yrb[1 - half, g].astype(F32)
            )

    def q_copy(half):
        return remote(qs.at[half], qr.at[half], q_s.at[half], q_r.at[half], across, col)

    def sent():
        for half in range(2):
            feat_across(half).wait_send()
        for kind in range(3):
            for way in range(2):
                for g in range(2):
                    if (kind, g) != (0, 0):
                        feat_y(kind, way, g).wait_send()

        def sent_pair(u, carry):
            pair_copy(u).wait_send()
            sig_pair(u, k).wait_send()
            return carry

        lax.fori_loop(0, 16, sent_pair, 0)

        def sent_x(j, carry):
            for kind in range(3):
                for way in range(2):
                    x_copy(kind, way, j).wait_send()
                    sig_x(kind, way, j).wait_send()
            return carry

        lax.fori_loop(0, 4, sent_x, 0)
        for j in range(3):
            z_copy(j).wait_send()
        for piece in range(4):

            @pl.when((z < 3) & (piece <= z))
            def _():
                sig_z(0, piece).wait_send()

            @pl.when((z > 0) & (piece >= z))
            def _():
                sig_z(1, piece).wait_send()

        for step in range(1, 4):
            wa_copy((y + step) % 4, y).wait_send()
            wx_copy((x + step) % 4, x).wait_send()
            wd_copy((x + step) % 4, x).wait_send()
        for step in range(1, 8):
            wz_copy((place8 + step) % 8, place8).wait_send()
        wk_copy().wait_send()
        we_copy(k).wait_send()

    y_open(0)
    y_relay(0)
    y_open(1)
    weights_twin()
    y_close(0)
    for half in range(2):
        qs[half] = acc[y, 1 - h, rows(half), :].astype(BF16)
        q_copy(half).start()
    y_relay(1)
    y_close(1)
    weights_end()
    sent()
    for kind in range(3):
        for way in range(2):
            for g in range(2):
                y_copy(kind, way, g).wait_send()
    for step in range(1, 4):
        wg_copy((y + step) % 4, y).wait_send()
    output_store().wait()
    weight_store().wait()
    bias_store().wait()
    for half in range(2):
        q_copy(half).wait_recv()
        acc[y, h, rows(half), :] = acc[y, h, rows(half), :] + qr[half].astype(F32)
    features_out[...] = split_dot(acc[y, h].T, weight_in[...], (((1,), (1,)), ((), ()))).astype(BF16)
    features_store().start()


    for half in range(2):
        q_copy(half).wait_send()
    features_store().wait()


def hand_over(output, grad_features, grad_weight, grad_bias, output_to, features_to, weight_to, bias_to):
    output_to[...] = output[...]
    features_to[...] = grad_features[...]
    weight_to[...] = grad_weight[...]
    bias_to[...] = grad_bias[...]


def on_device(features, weight, bias_vector, adjacency_tiles, tile_index, tile_count, grad_output):
    vmem = pl.BlockSpec(memory_space=pltpu.VMEM)
    scalars = pl.BlockSpec(memory_space=pltpu.SMEM)
    anywhere = pl.BlockSpec(memory_space=pl.ANY)
    dma = pltpu.SemaphoreType.DMA
    output, grad_features, grad_weight, grad_bias = pl.pallas_call(
        kernel,
        out_shape=(
            jax.ShapeDtypeStruct((N, N), BF16),
            jax.ShapeDtypeStruct((N, N), BF16),
            jax.ShapeDtypeStruct((N, N), F32),
            jax.ShapeDtypeStruct((1, N), F32),
        ),
        in_specs=[
            scalars, scalars, anywhere, anywhere, anywhere, anywhere, anywhere,
        ],
        out_specs=(anywhere, anywhere, anywhere, anywhere),
        scratch_shapes=[
            pltpu.VMEM((SLOTS + 1, TILE, TILE), BF16),
            pltpu.VMEM((8 * N, N), BF16),
            pltpu.VMEM((16, N, N), BF16),
            pltpu.VMEM((16, N, N), BF16),
            pltpu.VMEM((4, N, N), BF16),
            pltpu.VMEM((2, 4, HALF, N), BF16),
            pltpu.VMEM((2, 4, HALF, N), BF16),
            pltpu.VMEM((2, 4, HALF, N), BF16),
            pltpu.VMEM((2, 4, HALF, N), BF16),
            pltpu.VMEM((2, 4, HALF, N), BF16),
            pltpu.VMEM((3, N, N), BF16),
            pltpu.VMEM((2, 4, N, N), BF16),
            pltpu.VMEM((16, 2, N, N), BF16),
            pltpu.VMEM((4, 2, N, N), F32),
            pltpu.VMEM((2, N, N), BF16),
            pltpu.VMEM((2, 2, HALF, N), BF16),
            pltpu.VMEM((2, 2, HALF, N), BF16),
            pltpu.VMEM((2, 2, HALF, N), BF16),
            pltpu.VMEM((2, 2, HALF, N), BF16),
            pltpu.VMEM((2, 2, HALF, N), BF16),
            pltpu.VMEM((2, HALF, N), BF16),
            pltpu.VMEM((2, HALF, N), BF16),
            pltpu.VMEM((4, 2, 4, 8, N + HALF), F32),
            pltpu.VMEM((4, 2, 4, 8, N + HALF), F32),
            pltpu.VMEM((2, 4, 8, N + HALF), F32),
            pltpu.VMEM((4, 8, N + HALF), F32),
            pltpu.VMEM((4, 8, N + HALF), F32),
            pltpu.VMEM((4, 8, N + HALF), F32),
            pltpu.VMEM((8, 8, N + HALF), F32),
            pltpu.VMEM((4, 8, N), F32),
            pltpu.VMEM((2, 4, 8, N), F32),
            pltpu.VMEM((4, 2, 4, 8, N), F32),
            pltpu.VMEM((N, N), BF16),
            pltpu.VMEM((16, 2, N, N), F32),
            pltpu.VMEM((N, N), BF16),
            pltpu.VMEM((1, N), F32),
            pltpu.VMEM((N, N), BF16),
            pltpu.VMEM((N, N), BF16),
            pltpu.VMEM((N, N), BF16),
            pltpu.VMEM((N, N), F32),
            pltpu.VMEM((1, N), F32),
            dma((LOADS,)),
            dma((3, 2, 2)), dma((3, 2, 2)), dma((2,)), dma((2,)),
            dma((16,)), dma((16,)), dma((3, 2, 4)), dma((3, 2, 4)), dma((3,)), dma((2, 4)),
            dma((16,)), dma((16,)), dma((3, 2, 4)), dma((3, 2, 4)), dma((2, 4)), dma((2, 4)),
            dma((3, 2, 2)), dma((3, 2, 2)), dma((2,)), dma((2,)),
            dma((4,)), dma((4,)), dma((1,)), dma((1,)), dma((4,)), dma((4,)), dma((8,)), dma((8,)),
            dma((4,)), dma((4,)), dma((1,)), dma((1,)), dma((4,)), dma((4,)), dma((4,)), dma((4,)),
            pltpu.SMEM((64,), jnp.int32),
        ],
        compiler_params=pltpu.CompilerParams(
            collective_id=0, has_side_effects=True, vmem_limit_bytes=56 * 1024 * 1024
        ),
        name="graph_layer",
    )(tile_index[0, 0], tile_count[0], features, weight, bias_vector[None, :], adjacency_tiles[0, 0], grad_output)
    output, grad_features, grad_weight, grad_bias = pl.pallas_call(
        hand_over,
        out_shape=(
            jax.ShapeDtypeStruct((N, N), BF16),
            jax.ShapeDtypeStruct((N, N), BF16),
            jax.ShapeDtypeStruct((N, N), F32),
            jax.ShapeDtypeStruct((1, N), F32),
        ),
        in_specs=[vmem, vmem, vmem, vmem],
        out_specs=(vmem, vmem, vmem, vmem),
        name="hand_over",
    )(output, grad_features, grad_weight, grad_bias)
    return output, grad_features, grad_weight, grad_bias[0]


def solution(mesh):
    return jax.shard_map(
        on_device,
        mesh=mesh,
        in_specs=(
            P(("col", "row"), None),
            P(),
            P(),
            P("row", "col", None, None, None),
            P("row", "col", None),
            P("row", "col"),
            P(("row", "col"), None),
        ),
        out_specs=(P(("row", "col"), None), P(("col", "row"), None), P(), P()),
        check_vma=False,
    )
```
